32 devices in a mesh: groups: 2 (over x), space: 8 (over z, y), rep: 2 (over core).
Axes of the slice: x: 2, y: 2, z: 4, core: 2. Of those that a mesh axis runs over, the one named last changes fastest.
Arguments:
- features: bfloat16 [2, 64, 8, 8, 512], P('rep', ('groups', 'space')), parts along dimension 1, may hold values from -6 to 6
- weight_one: bfloat16 [27, 64, 64], replicated, may hold values from -0.15625 to 0.15625
- weight_two: bfloat16 [27, 64, 64], replicated, may hold values from -0.15625 to 0.15625
- grad_out: bfloat16 [2, 64, 8, 8, 512], P('rep', ('groups', 'space')), parts along dimension 1, may hold values from -0.125 to 0.125
- active: int32 [2, 64, 512], P('rep', ('groups', 'space')), parts along dimension 1, may hold values 0 or 1
- send_list: int32 [2, 16, 8, 2], P('rep', ('groups', 'space')), parts along dimension 1, may hold values from 0 to 4, as said below
- local_nbr: int32 [2, 64, 27], P('rep', ('groups', 'space')), parts along dimension 1, may hold values from 0 to 20, as said below
Outputs:
- output: bfloat16 [2, 64, 8, 8, 512], P('rep', ('groups', 'space')), parts along dimension 1
- grad_one: float32 [54, 64, 64], P('groups'), parts along dimension 0
- grad_two: float32 [54, 64, 64], P('groups'), parts along dimension 0
The draws below stay inside these ranges and needn't reach their ends.
There are 2 independent parts, one for each index of `groups`. The reference program is written for one: setup_inputs(seed, part) draws one part's arguments, and reference() takes and returns one part's arrays. A program takes and returns all parts, laid end to end along the dimension named above; an argument that names none is the same for every part. Nothing has to cross between parts.
Inputs may be any that keep to these rules, and one draw needn't show every extreme that they name: Owners form two rows of 4: owner o is in row o // 4 at column o % 4. send_list[r, o, k, :] lists distinct local indices (below 4) of o's bricks that owner o + delta[k] reads, then the padding 4. Real bricks go only to an owner of the same row at column distance one, or of the other row at column distance at most one, so every entry is 4 where o + delta[k] is no such owner; the two owners of a column send each other exactly 2 bricks. local_nbr[r, n, d] indexes the table of the owner o of brick n: below 4 one of o's bricks, 4 + k * 2 + s the brick of send_list[r, o - delta[k], k, s], and 20 the empty brick. Entries of the middle kind name only slots that hold a real brick; direction 13 names the brick itself.
All inputs are finite; a program needn't handle non-finite values. No bound on the sum of `active` on one device may be relied on, other than what follows from the above.
Results may differ from the reference program's by a relative error of at most 0.005.
Values may be sent and summed in bfloat16 or wider, within the bound.
A program may use at most 128 MiB of HBM per device.

```python
import jax
import jax.numpy as jnp
from jax import lax

C = 64
BE = 8
BR = 4
SLOTS = 2
BRICKS = 32
N_SPACE = 8
N_REP = 2


def neighbour_plan(key):
    half_count = N_SPACE // 2
    owner_ids = jnp.arange(N_SPACE, dtype=jnp.int32)
    row_now = owner_ids // half_count
    col_now = owner_ids % half_count
    left_ok = col_now > 0
    right_ok = col_now < half_count - 1
    top_row = row_now == 0
    low_row = row_now == 1
    usable = jnp.stack([left_ok, right_ok, top_row & left_ok, top_row, top_row & right_ok, low_row & left_ok, low_row, low_row & right_ok], axis=1)
    across = ((jnp.arange(8, dtype=jnp.int32) == 3) | (jnp.arange(8, dtype=jnp.int32) == 6))[None, None, :]
    counts = jax.random.randint(jax.random.fold_in(key, 101), (N_REP, N_SPACE, 8), 1, SLOTS + 1)
    counts = jnp.where(across, SLOTS, counts)
    counts = jnp.where(usable[None], counts, 0).astype(jnp.int32)
    starts = jax.random.randint(jax.random.fold_in(key, 102), (N_REP, N_SPACE, 8), 0, BR)
    starts = jnp.where(across, 0, starts).astype(jnp.int32)
    deltas = jnp.array([-1, 1, half_count - 1, half_count, half_count + 1, -half_count - 1, -half_count, 1 - half_count], jnp.int32)
    return (deltas, counts, starts)


def draw_send_list(key, part):
    deltas, counts, starts = neighbour_plan(key)
    slot_ids = jnp.arange(SLOTS, dtype=jnp.int32)
    values = jnp.where(slot_ids[None, None, None, :] < counts[..., None], (starts[..., None] + slot_ids) % BR, BR)
    return values.astype(jnp.int32)


def draw_local_nbr(key, part):
    deltas, counts, starts = neighbour_plan(key)
    key = jax.random.fold_in(key, 9)
    owner_ids = jnp.arange(N_SPACE, dtype=jnp.int32)
    senders = owner_ids[:, None] - deltas[None, :]
    inside = (senders >= 0) & (senders < N_SPACE)
    clipped = jnp.clip(senders, 0, N_SPACE - 1)
    recv_counts = counts[:, clipped, jnp.arange(8, dtype=jnp.int32)[None, :]]
    recv_counts = jnp.where(inside[None], recv_counts, 0)
    zero_row = BR + 8 * SLOTS
    drawn = jax.random.randint(key, (N_REP, N_SPACE, BR, 27), 0, BR + 8 * SLOTS + 2)
    kind_of = jnp.clip((drawn - BR) // SLOTS, 0, 7)
    slot_of = (drawn - BR) % SLOTS
    rep_grid = jnp.arange(N_REP, dtype=jnp.int32)[:, None, None, None]
    owner_grid = owner_ids[None, :, None, None]
    slot_limit = recv_counts[rep_grid, owner_grid, kind_of]
    in_range = (drawn >= BR) & (drawn < BR + 8 * SLOTS) & (slot_of < slot_limit)
    result = jnp.where(drawn < BR, drawn, jnp.where(in_range, drawn, zero_row))
    result = result.at[:, :, :, 13].set(jnp.arange(BR, dtype=jnp.int32)[None, None, :])
    result = result.at[:, :, 0, 0].set(zero_row)
    return result.reshape(N_REP, BRICKS, 27).astype(jnp.int32)


def plant(values, own_key, least, high):
    longest = values.shape.index(max(values.shape))
    spots = []
    for shift in (0, 1):
        where = [jax.random.randint(jax.random.fold_in(own_key, axis), (), 0, length) for axis, length in enumerate(values.shape)]
        where[longest] = (where[longest] + shift) % values.shape[longest]
        spots.append(tuple(where))
    return values.at[spots[0]].set(least).at[spots[1]].set(high)


def steps_of(own_key, extent, shards, smallest, largest):
    gain, own = 1.0, jax.random.fold_in(own_key, 6)
    for dim, blocks in shards:
        heights = jnp.exp(jax.random.uniform(jax.random.fold_in(own, dim), (blocks,), jnp.float32, smallest / len(shards), largest / len(shards)))
        gain = gain * jnp.repeat(heights, extent[dim] // blocks).reshape([-1 if axis == dim else 1 for axis in range(len(extent))])
    return gain


def noise(stream_key, shape, width, limit, shards=(), kind=jnp.bfloat16):
    level = steps_of(stream_key, shape, shards, -0.22, 0.18) if shards else 1.0
    values = jax.random.normal(stream_key, shape, jnp.float32) * width * level
    return jnp.minimum(jnp.maximum(values, -limit), limit).astype(kind)


def setup_inputs(seed: int = 0, part: int = 0) -> dict:
    seeds = jax.random.split(jax.random.key(seed), 8)
    part_splits = jax.random.split(jax.random.fold_in(seeds[7], part), 8)
    return {
        "features": noise(part_splits[0], (N_REP, BRICKS, BE, BE, BE * C), 1.0, 6.0, ((0, 2), (1, 8))),
        "weight_one": noise(seeds[1], (27, C, C), (27 * C) ** -0.5, 0.15625),
        "weight_two": noise(seeds[2], (27, C, C), (27 * C) ** -0.5, 0.15625),
        "grad_out": noise(part_splits[3], (N_REP, BRICKS, BE, BE, BE * C), (1.0 / (N_REP * BRICKS * 256) ** 0.5), 0.125, ((0, 2), (1, 8))),
        "active": plant((jax.random.randint(part_splits[4], (N_REP, BRICKS, BE * BE * BE), 0, 5) < 3).astype(jnp.int32), jax.random.fold_in(part_splits[4], 1), 0, 1),
        "send_list": draw_send_list(jax.random.fold_in(jax.random.fold_in(seeds[7], part), 71), part),
        "local_nbr": draw_local_nbr(jax.random.fold_in(jax.random.fold_in(seeds[7], part), 71), part),
    }


def offset_list():
    return [(a, b, c) for a in (-1, 0, 1) for b in (-1, 0, 1) for c in (-1, 0, 1)]

def source_span(offset):
    if offset < 0:
        return slice(BE - 1, BE)
    if offset > 0:
        return slice(0, 1)
    return slice(0, BE)

def padded_span(offset):
    if offset < 0:
        return slice(0, 1)
    if offset > 0:
        return slice(BE + 1, BE + 2)
    return slice(1, BE + 1)

def assemble(brick_table, neighbours):
    pieces = {}
    for direction, offset in enumerate(offset_list()):
        window = (slice(None),) + tuple((source_span(s) for s in offset))
        pieces[offset] = jnp.take(brick_table[window], neighbours[:, direction], axis=0)
    planes = []
    for a in (-1, 0, 1):
        strips = [jnp.concatenate([pieces[a, b, c] for c in (-1, 0, 1)], axis=3) for b in (-1, 0, 1)]
        planes.append(jnp.concatenate(strips, axis=2))
    return jnp.concatenate(planes, axis=1)

def unfold(padded, facing, length):
    blocks = []
    for offset in offset_list():
        corner = [1 + facing * s for s in offset]
        blocks.append(padded[:, corner[0]:corner[0] + length, corner[1]:corner[1] + length, corner[2]:corner[2] + length])
    stacked = jnp.concatenate(blocks, axis=-1)
    return stacked.reshape(-1, stacked.shape[-1])

def convolve(brick_table, neighbours, weight):
    unfolded = unfold(assemble(brick_table, neighbours), 1, BE)
    kernel = weight.reshape(-1, weight.shape[2])
    return (jnp.dot(unfolded, kernel, preferred_element_type=jnp.float32), unfolded)

def spread_back(gradient, weight):
    widened = jnp.pad(gradient, ((0, 0), (2, 2), (2, 2), (2, 2), (0, 0)))
    unfolded = unfold(widened, -1, BE + 2)
    kernel = jnp.transpose(weight, (0, 2, 1)).reshape(-1, weight.shape[1])
    result = jnp.dot(unfolded, kernel, preferred_element_type=jnp.float32)
    return result.reshape((gradient.shape[0], BE + 2, BE + 2, BE + 2, weight.shape[1]))

def deposit(totals, spread, neighbours):
    for direction, offset in enumerate(offset_list()):
        source = (slice(None),) + tuple((padded_span(s) for s in offset))
        target_box = tuple((source_span(s) for s in offset))
        totals = totals.at[(neighbours[:, direction],) + target_box].add(spread[source])
    return totals

def weight_grad(unfolded, gradient, shape):
    total = lax.dot_general(unfolded, gradient, (((0,), (0,)), ((), ())), preferred_element_type=jnp.float32)
    return total.reshape(shape)

def silu_slope(values):
    logistic = jax.nn.sigmoid(values)
    return logistic * (1.0 + values * (1.0 - logistic))

def reference(features, weight_one, weight_two, grad_out, active, send_list, local_nbr):
    brick_shape = (BE, BE, BE, C)
    half_count = N_SPACE // 2
    deltas = jnp.array([-1, 1, half_count - 1, half_count, half_count + 1, -half_count - 1, -half_count, 1 - half_count], jnp.int32)
    owner_ids = jnp.arange(N_SPACE, dtype=jnp.int32)
    senders = owner_ids[:, None] - deltas[None, :]
    inside = (senders >= 0) & (senders < N_SPACE)
    clipped = jnp.clip(senders, 0, N_SPACE - 1).astype(jnp.int32)
    direction_ids = jnp.arange(8, dtype=jnp.int32)[None, :]
    empty_brick = jnp.zeros((1,) + brick_shape, jnp.bfloat16)
    grad_one = jnp.zeros(weight_one.shape, jnp.float32)
    grad_two = jnp.zeros(weight_two.shape, jnp.float32)
    outputs = []
    for replica in range(N_REP):
        mask_full = active[replica].reshape((BRICKS, BE, BE, BE, 1)).astype(jnp.float32)
        mask_half = active[replica].reshape((BRICKS, BE, BE, BE, 1)).astype(jnp.bfloat16)
        inputs = features[replica].reshape((BRICKS,) + brick_shape) * mask_half
        routes = send_list[replica]
        entries = routes[clipped, direction_ids]
        valid = inside[:, :, None] & (entries < BR)
        incoming = jnp.where(valid, clipped[:, :, None] * BR + entries, BRICKS).astype(jnp.int32)
        incoming = incoming.reshape(N_SPACE, 8 * SLOTS)
        local_ids = owner_ids[:, None] * BR + jnp.arange(BR, dtype=jnp.int32)[None, :]
        mapping = jnp.concatenate([local_ids, incoming, jnp.full((N_SPACE, 1), BRICKS, jnp.int32)], axis=1)
        lookup = jnp.take_along_axis(mapping, local_nbr[replica].reshape(N_SPACE, BR * 27), axis=1)
        lookup = lookup.reshape(N_SPACE, BR, 27)
        first_table = jnp.concatenate([inputs, empty_brick], axis=0)

        def first_layer(owner_nbr):
            return convolve(first_table, owner_nbr, weight_one)[0]
        pre_one = lax.map(first_layer, lookup).reshape((BRICKS,) + brick_shape)
        hidden = (mask_full * jax.nn.silu(pre_one)).astype(jnp.bfloat16)
        second_table = jnp.concatenate([hidden, empty_brick], axis=0)
        upstream = grad_out[replica].reshape((BRICKS,) + brick_shape) * mask_half
        up_blocks = upstream.reshape((N_SPACE, BR) + brick_shape)

        def second_layer(brick_items):
            result, unfolded = convolve(second_table, brick_items[0], weight_two)
            return (result, weight_grad(unfolded, brick_items[1].reshape(-1, C), weight_two.shape))
        pre_two, grad_parts = lax.map(second_layer, (lookup, up_blocks))
        grad_two = grad_two + lax.optimization_barrier(jnp.sum(grad_parts, axis=0))
        output = (mask_full * pre_two.reshape((BRICKS,) + brick_shape)).astype(jnp.bfloat16)
        outputs.append(output.reshape(features.shape[1:]))

        def spread_step(totals, brick_items):
            return (deposit(totals, spread_back(brick_items[1], weight_two), brick_items[0]), None)
        start_totals = jnp.zeros((BRICKS + 1,) + brick_shape, jnp.float32)
        totals, unused = lax.scan(spread_step, start_totals, (lookup, up_blocks))
        inner_grad = (mask_full * totals[:BRICKS] * silu_slope(pre_one)).astype(jnp.bfloat16)

        def first_grads(brick_items):
            unfolded = unfold(assemble(first_table, brick_items[0]), 1, BE)
            return weight_grad(unfolded, brick_items[1].reshape(-1, C), weight_one.shape)
        grad_parts = lax.map(first_grads, (lookup, inner_grad.reshape((N_SPACE, BR) + brick_shape)))
        grad_one = grad_one + lax.optimization_barrier(jnp.sum(grad_parts, axis=0))
    return (jnp.stack(outputs, axis=0), grad_one, grad_two)
```

```python
import functools

import jax
import jax.numpy as jnp
from jax import lax
from jax.experimental import pallas as pl
from jax.experimental.pallas import tpu as pltpu
from jax.sharding import PartitionSpec as P

BE = 8
F32 = jnp.float32
BF16 = jnp.bfloat16
LIMIT = 48 * 1024 * 1024
VM = pl.BlockSpec(memory_space=pltpu.VMEM)
SM = pl.BlockSpec(memory_space=pltpu.SMEM)


def from_behind(value, axis, steps):
    count = lax.axis_size(axis)
    initial, last = (max(0, -steps), min(count, count - steps))
    return lax.ppermute(value, axis, [(source, source + steps) for source in range(initial, last)])


def iota(shape, dim):
    return lax.broadcasted_iota(jnp.int32, shape, dim)


def expand_mask(mask_ref):
    rows, edge = mask_ref.shape
    width = edge * 64
    spread = (iota((edge, width), 1) // 64 == iota((edge, width), 0)).astype(BF16)
    wide = jnp.dot(mask_ref[...].astype(BF16), spread, preferred_element_type=F32)
    return wide.reshape(BE, rows // BE, width)


def to_rows(ref):
    return jnp.concatenate([ref[b].astype(F32) for b in range(ref.shape[0])], axis=1)


def fill_outbound(send_ref, bricks_ref, out_refs):
    last = bricks_ref.shape[0] - 1
    for k, out in enumerate(out_refs):
        for s in range(out.shape[0]):
            out[s] = bricks_ref[jnp.minimum(send_ref[k, s], last)]


def fill_table(table_ref, own_ref, received):
    bricks = own_ref.shape[0]
    table_ref[0:bricks] = own_ref[...]
    row = bricks
    for ref in received:
        count = ref.shape[0]
        table_ref[row : row + count] = ref[...]
        row += count
    table_ref[row] = jnp.zeros(table_ref.shape[1:], table_ref.dtype)


def assemble(table_ref, nbr_ref, shifted_ref):
    width = table_ref.shape[3]
    lanes = iota((BE, 128), 1)
    rows = iota((BE, width + 128), 0)

    def plane(b, direction, source):
        strips = []
        for j in range(3):
            first = direction + 3 * j
            mid = table_ref[nbr_ref[b, first + 1], source].astype(F32)
            low = table_ref[nbr_ref[b, first], source, :, width - 128 : width].astype(F32)
            high = table_ref[nbr_ref[b, first + 2], source, :, 0:128].astype(F32)
            end = mid[:, width - 128 :]
            body = jnp.concatenate(
                [mid[:, : width - 128], jnp.where(lanes >= 64, low, end)], axis=1
            )
            tail = jnp.where(lanes < 64, high, end)
            strips.append(
                jnp.concatenate([pltpu.roll(body, 64, 1), pltpu.roll(tail, 64, 1)], axis=1)
            )
        before = pltpu.roll(jnp.where(rows == BE - 1, strips[0], strips[1]), 1, 0)
        after = pltpu.roll(jnp.where(rows == 0, strips[2], strips[1]), BE - 1, 0)
        return before, strips[1], after

    def step(x, carry):
        side = jnp.where(x == 0, 0, jnp.where(x == BE + 1, 2, 1))
        source = lax.rem(x + BE - 1, BE)
        for pair in range(nbr_ref.shape[0] // 2):
            one = plane(2 * pair, 9 * side, source)
            two = plane(2 * pair + 1, 9 * side, source)
            for j in range(3):
                both = jnp.concatenate([one[j], two[j]], axis=0).astype(BF16)
                shifted_ref[j, x, 16 * pair : 16 * pair + 16, :] = both
        return carry

    lax.fori_loop(0, BE + 2, step, 0)


def banded_conv(shifted_ref, kernel_ref, result_ref):
    length, rows, width = result_ref.shape

    def step(p, carry):
        at = pl.multiple_of(p * 128, 128)
        total = jnp.zeros((length * rows, 128), F32)
        for i in range(3):
            for j in range(3):
                block = shifted_ref[j, i : i + length, :, pl.ds(at, 256)]
                total = total + jnp.dot(
                    block.reshape(length * rows, 256),
                    kernel_ref[3 * i + j],
                    preferred_element_type=F32,
                )
        result_ref[:, :, pl.ds(at, 128)] = total.reshape(length, rows, 128)
        return carry

    lax.fori_loop(0, width // 128, step, 0)


def banded_grad(shifted_ref, upward, grad_ref):
    rows, width = upward.shape
    turned = [
        upward[:, 128 * p : 128 * p + 128].T.astype(BF16) for p in range(width // 128)
    ]

    def step(i, carry):
        for j in range(3):
            total = jnp.zeros((128, 256), F32)
            for p in range(width // 128):
                block = shifted_ref[j, pl.ds(i, BE), :, 128 * p : 128 * p + 256]
                total = total + jnp.dot(
                    turned[p], block.reshape(rows, 256), preferred_element_type=F32
                )
            flat = total.T
            for k in range(3):
                grad_ref[9 * i + 3 * j + k] = (
                    flat[64 * k : 64 * k + 64, 0:64] + flat[64 * k + 64 : 64 * k + 128, 64:128]
                )
        return carry

    lax.fori_loop(0, 3, step, 0)


def mask_kernel(send_ref, features_ref, mask_ref, x_ref, *out_refs):
    wide = expand_mask(mask_ref)
    for b in range(x_ref.shape[0]):
        part = wide[:, BE * b : BE * b + BE, :]
        x_ref[b] = (features_ref[b].astype(F32) * part).astype(BF16)
    fill_outbound(send_ref, x_ref, out_refs)


def spread_kernel(nbr_ref, up_ref, mask_ref, kernel_ref, own_ref, *rest):
    out_refs, (shifted_ref, spread_ref, totals_ref) = rest[:-3], rest[-3:]
    bricks, width = own_ref.shape[0], own_ref.shape[3]
    wide = expand_mask(mask_ref)
    up = (to_rows(up_ref) * wide).astype(BF16).astype(F32)
    for j in range(3):
        for x in (0, 1, BE + 2, BE + 3):
            shifted_ref[j, x] = jnp.zeros(shifted_ref.shape[2:], BF16)
    for x in range(BE):
        for b in range(bricks):
            tile = up[x, BE * b : BE * b + BE, :]
            side = jnp.zeros((BE, 128), F32)
            tile = jnp.concatenate([side, tile, side], axis=1)
            tile = jnp.concatenate([tile, jnp.zeros_like(tile)], axis=0)
            for j in range(3):
                moved = pltpu.roll(tile, 2 - j, 0) if j < 2 else tile
                shifted_ref[j, x + 2, 16 * b : 16 * b + 16, :] = moved.astype(BF16)
    banded_conv(shifted_ref, kernel_ref, spread_ref)

    def clear(t, carry):
        totals_ref[t] = jnp.zeros(totals_ref.shape[1:], F32)
        return carry

    lax.fori_loop(0, totals_ref.shape[0], clear, 0)
    lanes = iota((BE, 128), 1)
    rows = iota((BE, width), 0)
    rows_short = iota((BE, 128), 0)

    def deposit(x, carry):
        side = jnp.where(x == 0, 0, jnp.where(x == BE + 1, 2, 1))
        target = lax.rem(x + BE - 1, BE)
        for b in range(bricks):
            tile = spread_ref[x, 16 * b : 16 * b + 16, :]
            tile = pltpu.roll(pltpu.roll(tile, width + 64, 1), 15, 0)
            for j in range(3):
                first = 9 * side + 3 * j
                body = tile[0:BE, 0:width] if j == 1 else tile[BE : 2 * BE, 0:width]
                ends = tile[0:BE, width:] if j == 1 else tile[BE : 2 * BE, width:]
                if j != 1:
                    keep = BE - 1 if j == 0 else 0
                    body = jnp.where(rows == keep, body, 0.0)
                    ends = jnp.where(rows_short == keep, ends, 0.0)
                totals_ref[nbr_ref[b, first + 1], target] += body
                totals_ref[nbr_ref[b, first], target, :, width - 128 : width] += jnp.where(
                    lanes >= 64, ends, 0.0
                )
                totals_ref[nbr_ref[b, first + 2], target, :, 0:128] += jnp.where(
                    lanes < 64, ends, 0.0
                )
        return carry

    lax.fori_loop(0, BE + 2, deposit, 0)
    own_ref[...] = totals_ref[0:bricks]
    row = bricks
    for out in out_refs:
        count = out.shape[0]
        out[...] = totals_ref[row : row + count].astype(BF16)
        row += count


def first_kernel(count, send_ref, nbr_ref, x_ref, mask_ref, kernel_ref, *rest):
    received, rest = rest[:count], rest[count:]
    pre_ref, shifted_ref, hidden_ref = rest[:3]
    out_refs, (table_ref,) = rest[3:-1], rest[-1:]
    fill_table(table_ref, x_ref, received)
    assemble(table_ref, nbr_ref, shifted_ref)
    banded_conv(shifted_ref, kernel_ref, pre_ref)
    pre = pre_ref[...]
    hidden = expand_mask(mask_ref) * (pre * jax.nn.sigmoid(pre))
    for b in range(hidden_ref.shape[0]):
        hidden_ref[b] = hidden[:, BE * b : BE * b + BE, :].astype(BF16)
    fill_outbound(send_ref, hidden_ref, out_refs)


def inner_kernel(send_ref, mask_ref, pre_ref, shifted_ref, own_ref, *rest):
    received, (grad_ref, home_ref) = rest[:-2], rest[-2:]
    bricks = own_ref.shape[0]
    home_ref[0:bricks] = own_ref[...]
    for k, ref in enumerate(received):
        for s in range(ref.shape[0]):
            home_ref[send_ref[k, s]] += ref[s].astype(F32)
    back = jnp.concatenate([home_ref[b] for b in range(bricks)], axis=1)
    pre = pre_ref[...]
    logistic = jax.nn.sigmoid(pre)
    slope = logistic * (1.0 + pre * (1.0 - logistic))
    inner = (expand_mask(mask_ref) * back * slope).astype(BF16).astype(F32)
    banded_grad(shifted_ref, inner.reshape(-1, inner.shape[2]), grad_ref)


def second_kernel(nbr_ref, hidden_ref, up_ref, mask_ref, kernel_ref, *rest):
    received, (output_ref, grad_ref, table_ref, shifted_ref, post_ref) = rest[:-5], rest[-5:]
    fill_table(table_ref, hidden_ref, received)
    assemble(table_ref, nbr_ref, shifted_ref)
    wide = expand_mask(mask_ref)
    up = (to_rows(up_ref) * wide).astype(BF16).astype(F32)
    banded_grad(shifted_ref, up.reshape(-1, up.shape[2]), grad_ref)
    banded_conv(shifted_ref, kernel_ref, post_ref)
    post = post_ref[...] * wide
    for b in range(output_ref.shape[0]):
        output_ref[b] = post[:, BE * b : BE * b + BE, :].astype(BF16)


def banded(weight):
    split = weight.reshape(9, 3, 64, 64)
    left = jnp.pad(split, ((0, 0), (0, 1), (0, 0), (0, 0)))
    right = jnp.pad(split, ((0, 0), (1, 0), (0, 0), (0, 0)))
    return jnp.concatenate([left, right], axis=-1).reshape(9, 256, 128)


def call(body, specs, outs, scratch, args):
    return pl.pallas_call(
        body,
        out_shape=outs,
        in_specs=specs,
        out_specs=[VM] * len(outs),
        scratch_shapes=scratch,
        compiler_params=pltpu.CompilerParams(vmem_limit_bytes=LIMIT),
    )(*args)


def per_device(features, weight_one, weight_two, grad_out, active, send_list, local_nbr):
    bricks = features.shape[1]
    width = features.shape[4]
    brick = features.shape[2:]
    send = send_list[0, 0]
    nbr = local_nbr[0]
    owners = lax.axis_size("space")
    slots = send.shape[1]
    half = owners // 2
    deltas = [-1, 1, half - 1, half, half + 1, -half - 1, -half, 1 - half]
    mask = active[0].reshape(bricks, BE, BE, BE).transpose(1, 0, 2, 3).reshape(-1, BE)
    mask = mask.astype(F32)
    kernel_one = banded(weight_one)
    kernel_two = banded(weight_two)
    kernel_back = banded(jnp.flip(weight_two, 0).transpose(0, 2, 1))

    shape = jax.ShapeDtypeStruct
    outbound = [shape((slots,) + brick, BF16)] * len(deltas)
    bricks_half = shape((bricks,) + brick, BF16)
    bricks_full = shape((bricks,) + brick, F32)
    entries = bricks + len(deltas) * slots + 1
    rows = bricks * BE
    table = pltpu.VMEM((entries,) + brick, BF16)
    shifted = (3, BE + 2, rows, width + 128)
    grads = shape(weight_one.shape, F32)
    pre_shape = (BE, rows, width)

    x, *sends = call(
        mask_kernel, [SM, VM, VM], [bricks_half] + outbound, [], (send, features[0], mask)
    )
    x_in = [from_behind(v, "space", d) for v, d in zip(sends, deltas)]
    own_back, *sends = call(
        spread_kernel,
        [SM, VM, VM, VM],
        [bricks_full] + outbound,
        [
            pltpu.VMEM((3, BE + 4, 16 * bricks, width + 256), BF16),
            pltpu.VMEM((BE + 2, 16 * bricks, width + 128), F32),
            pltpu.VMEM((entries,) + brick, F32),
        ],
        (nbr, grad_out[0], mask, kernel_back),
    )
    back_in = [from_behind(v, "space", -d) for v, d in zip(sends, deltas)]
    pre, windows, hidden, *sends = call(
        functools.partial(first_kernel, len(deltas)),
        [SM, SM] + [VM] * (3 + len(deltas)),
        [shape(pre_shape, F32), shape(shifted, BF16), bricks_half] + outbound,
        [table],
        (send, nbr, x, mask, kernel_one, *x_in),
    )
    hidden_in = [from_behind(v, "space", d) for v, d in zip(sends, deltas)]
    (grad_one,) = call(
        inner_kernel,
        [SM] + [VM] * (4 + len(deltas)),
        [grads],
        [pltpu.VMEM((bricks + 1,) + brick, F32)],
        (send, mask, pre, windows, own_back, *back_in),
    )
    output, grad_two = call(
        second_kernel,
        [SM] + [VM] * (4 + len(deltas)),
        [bricks_half, grads],
        [table, pltpu.VMEM(shifted, BF16), pltpu.VMEM(pre_shape, F32)],
        (nbr, hidden, grad_out[0], mask, kernel_two, *hidden_in),
    )
    grad_one = lax.psum(grad_one, ("space", "rep"))
    grad_two = lax.psum(grad_two, ("space", "rep"))
    return (output.reshape(features.shape), grad_one, grad_two)


def solution(mesh):
    in_specs = (
        P("rep", ("groups", "space"), None, None, None),
        P(),
        P(),
        P("rep", ("groups", "space"), None, None, None),
        P("rep", ("groups", "space"), None),
        P("rep", ("groups", "space"), None, None),
        P("rep", ("groups", "space"), None),
    )
    out_specs = (
        P("rep", ("groups", "space"), None, None, None),
        P("groups", None, None),
        P("groups", None, None),
    )
    return jax.shard_map(
        per_device, mesh=mesh, in_specs=in_specs, out_specs=out_specs, check_vma=False
    )
```

```python
import functools

import jax
import jax.numpy as jnp
from jax import lax
from jax.experimental import pallas as pl
from jax.experimental.pallas import tpu as pltpu
from jax.sharding import PartitionSpec as P

BE = 8
F32 = jnp.float32
BF16 = jnp.bfloat16
LIMIT = 48 * 1024 * 1024
VM = pl.BlockSpec(memory_space=pltpu.VMEM)
SM = pl.BlockSpec(memory_space=pltpu.SMEM)


def iota(shape, dim):
    return lax.broadcasted_iota(jnp.int32, shape, dim)


def expand_mask(mask_ref):
    rows, edge = mask_ref.shape
    width = edge * 64
    spread = (iota((edge, width), 1) // 64 == iota((edge, width), 0)).astype(BF16)
    wide = jnp.dot(mask_ref[...].astype(BF16), spread, preferred_element_type=F32)
    return wide.reshape(BE, rows // BE, width)


def to_rows(ref):
    return jnp.concatenate([ref[b].astype(F32) for b in range(ref.shape[0])], axis=1)


def fill_outbound(send_ref, bricks_ref, out_ref, bricks):
    slots = send_ref.shape[1]
    for k in range(send_ref.shape[0]):
        for s in range(slots):
            out_ref[slots * k + s] = bricks_ref[jnp.minimum(send_ref[k, s], bricks - 1)]


def assemble(table_ref, nbr_ref, shifted_ref):
    width = table_ref.shape[3]
    lanes = iota((BE, 128), 1)
    rows = iota((BE, width + 128), 0)

    def plane(b, direction, source):
        strips = []
        for j in range(3):
            first = direction + 3 * j
            mid = table_ref[nbr_ref[b, first + 1], source].astype(F32)
            low = table_ref[nbr_ref[b, first], source, :, width - 128 : width].astype(F32)
            high = table_ref[nbr_ref[b, first + 2], source, :, 0:128].astype(F32)
            end = mid[:, width - 128 :]
            body = jnp.concatenate(
                [mid[:, : width - 128], jnp.where(lanes >= 64, low, end)], axis=1
            )
            tail = jnp.where(lanes < 64, high, end)
            strips.append(
                jnp.concatenate([pltpu.roll(body, 64, 1), pltpu.roll(tail, 64, 1)], axis=1)
            )
        before = pltpu.roll(jnp.where(rows == BE - 1, strips[0], strips[1]), 1, 0)
        after = pltpu.roll(jnp.where(rows == 0, strips[2], strips[1]), BE - 1, 0)
        return before, strips[1], after

    def step(x, carry):
        side = jnp.where(x == 0, 0, jnp.where(x == BE + 1, 2, 1))
        source = lax.rem(x + BE - 1, BE)
        for pair in range(nbr_ref.shape[0] // 2):
            one = plane(2 * pair, 9 * side, source)
            two = plane(2 * pair + 1, 9 * side, source)
            for j in range(3):
                both = jnp.concatenate([one[j], two[j]], axis=0).astype(BF16)
                shifted_ref[j, x, 16 * pair : 16 * pair + 16, :] = both
        return carry

    lax.fori_loop(0, BE + 2, step, 0)


def banded_conv(shifted_ref, kernel_ref, result_ref):
    length, rows, width = result_ref.shape

    def step(p, carry):
        at = pl.multiple_of(p * 128, 128)
        total = jnp.zeros((length * rows, 128), F32)
        for i in range(3):
            for j in range(3):
                block = shifted_ref[j, i : i + length, :, pl.ds(at, 256)]
                total = total + jnp.dot(
                    block.reshape(length * rows, 256),
                    kernel_ref[3 * i + j],
                    preferred_element_type=F32,
                )
        result_ref[:, :, pl.ds(at, 128)] = total.reshape(length, rows, 128)
        return carry

    lax.fori_loop(0, width // 128, step, 0)


def banded_grad(shifted_ref, upward, grad_ref):
    rows, width = upward.shape
    turned = [
        upward[:, 128 * p : 128 * p + 128].T.astype(BF16) for p in range(width // 128)
    ]

    def step(i, carry):
        for j in range(3):
            total = jnp.zeros((128, 256), F32)
            for p in range(width // 128):
                block = shifted_ref[j, pl.ds(i, BE), :, 128 * p : 128 * p + 256]
                total = total + jnp.dot(
                    turned[p], block.reshape(rows, 256), preferred_element_type=F32
                )
            flat = total.T
            for k in range(3):
                block = (
                    flat[64 * k : 64 * k + 64, 0:64] + flat[64 * k + 64 : 64 * k + 128, 64:128]
                )
                at = pl.multiple_of(32 * (9 * i + 3 * j + k), 32)
                grad_ref[pl.ds(at, 32), :] = jnp.concatenate([block[0:32], block[32:64]], axis=1)
        return carry

    lax.fori_loop(0, 3, step, 0)


def spread_kernel(nbr_ref, up_ref, mask_ref, kernel_ref, own_ref, *rest):
    out_ref, shifted_ref, spread_ref, totals_ref = rest
    bricks, width = own_ref.shape[0], own_ref.shape[3]
    wide = expand_mask(mask_ref)
    up = (to_rows(up_ref) * wide).astype(BF16).astype(F32)
    for j in range(3):
        for x in (0, 1, BE + 2, BE + 3):
            shifted_ref[j, x] = jnp.zeros(shifted_ref.shape[2:], BF16)
    for x in range(BE):
        for b in range(bricks):
            tile = up[x, BE * b : BE * b + BE, :]
            side = jnp.zeros((BE, 128), F32)
            tile = jnp.concatenate([side, tile, side], axis=1)
            tile = jnp.concatenate([tile, jnp.zeros_like(tile)], axis=0)
            for j in range(3):
                moved = pltpu.roll(tile, 2 - j, 0) if j < 2 else tile
                shifted_ref[j, x + 2, 16 * b : 16 * b + 16, :] = moved.astype(BF16)
    banded_conv(shifted_ref, kernel_ref, spread_ref)

    def clear(t, carry):
        totals_ref[t] = jnp.zeros(totals_ref.shape[1:], F32)
        return carry

    lax.fori_loop(0, totals_ref.shape[0], clear, 0)
    lanes = iota((BE, 128), 1)
    rows = iota((BE, width), 0)
    rows_short = iota((BE, 128), 0)

    def deposit(x, carry):
        side = jnp.where(x == 0, 0, jnp.where(x == BE + 1, 2, 1))
        target = lax.rem(x + BE - 1, BE)
        for b in range(bricks):
            tile = spread_ref[x, 16 * b : 16 * b + 16, :]
            tile = pltpu.roll(pltpu.roll(tile, width + 64, 1), 15, 0)
            for j in range(3):
                first = 9 * side + 3 * j
                body = tile[0:BE, 0:width] if j == 1 else tile[BE : 2 * BE, 0:width]
                ends = tile[0:BE, width:] if j == 1 else tile[BE : 2 * BE, width:]
                if j != 1:
                    keep = BE - 1 if j == 0 else 0
                    body = jnp.where(rows == keep, body, 0.0)
                    ends = jnp.where(rows_short == keep, ends, 0.0)
                totals_ref[nbr_ref[b, first + 1], target] += body
                totals_ref[nbr_ref[b, first], target, :, width - 128 : width] += jnp.where(
                    lanes >= 64, ends, 0.0
                )
                totals_ref[nbr_ref[b, first + 2], target, :, 0:128] += jnp.where(
                    lanes < 64, ends, 0.0
                )
        return carry

    lax.fori_loop(0, BE + 2, deposit, 0)
    own_ref[...] = totals_ref[0:bricks]
    out_ref[...] = totals_ref[bricks : bricks + out_ref.shape[0]].astype(BF16)


def remote(source, target, sems, index, device):
    return pltpu.make_async_remote_copy(
        src_ref=source,
        dst_ref=target,
        send_sem=sems.at[0, index],
        recv_sem=sems.at[1, index],
        device_id=device,
        device_id_type=pl.DeviceIdType.MESH,
    )


class Halo:
    def __init__(self, owners, slots, sign, source, target, base, sems):
        half = owners // 2
        me = lax.axis_index("space")
        row, column = me // half, me % half
        self.sends, self.receives = [], []
        steps = [(0, -1), (0, 1), (1, -1), (1, 0), (1, 1), (-1, -1), (-1, 0), (-1, 1)]
        for k, (down, right) in enumerate(steps):
            down, right = sign * down, sign * right
            to_row, to_column = row + down, column + right
            from_row, from_column = row - down, column - right
            goes = (to_row >= 0) & (to_row < 2) & (to_column >= 0) & (to_column < half)
            comes = (from_row >= 0) & (from_row < 2) & (from_column >= 0) & (from_column < half)
            device = {"space": (me + down * half + right + owners) % owners}
            copy = remote(
                source.at[slots * k : slots * k + slots],
                target.at[base + slots * k : base + slots * k + slots],
                sems,
                k,
                device,
            )
            self.sends.append((goes, copy))
            self.receives.append((comes, copy))

    def start(self):
        for goes, copy in self.sends:
            pl.when(goes)(copy.start)

    def wait_recv(self):
        for comes, copy in self.receives:
            pl.when(comes)(copy.wait_recv)

    def wait_send(self):
        for goes, copy in self.sends:
            pl.when(goes)(copy.wait_send)


class Total:
    def __init__(self, owners, grad, pair_out, pair_in, mine, out, arrived, full, sems):
        self.owners = owners
        self.me = lax.axis_index("space")
        self.rep = lax.axis_index("rep")
        self.grad, self.pair_out, self.mine, self.out = grad, pair_out, mine, out
        self.pair_in, self.arrived, self.full = pair_in, arrived, full
        self.half = mine.shape[0]
        self.chunk = self.half // owners
        other = {"rep": 1 - self.rep}
        self.pair = remote(pair_out, pair_in, sems, 0, other)
        self.scatter, self.gather_out, self.gather_in = [], [], []
        own = full.at[self.rep, self.rows(self.me), :]
        for s in range(1, owners):
            there = (self.me + s) % owners
            device = {"space": there}
            self.scatter.append(
                remote(out.at[self.rows(there), :], arrived.at[s - 1], sems, s, device)
            )
            landing = full.at[self.rep, self.rows((self.me + owners - s) % owners), :]
            index = owners + s
            self.gather_out.append(remote(own, own, sems, index, device))
            self.gather_in.append(remote(landing, landing, sems, index, device))
        self.share = remote(full.at[self.rep], full.at[self.rep], sems, owners, other)
        coming = full.at[1 - self.rep]
        self.share_in = remote(coming, coming, sems, owners, other)

    def rows(self, owner):
        return pl.ds(pl.multiple_of(owner * self.chunk, self.chunk), self.chunk)

    def halves(self, rep):
        return pl.ds(pl.multiple_of(rep * self.half, self.half), self.half)

    def start_pair(self):
        self.pair_out[...] = self.grad[self.halves(1 - self.rep), :].astype(BF16)
        self.pair.start()

    def start_scatter(self):
        self.pair.wait_recv()
        total = self.grad[self.halves(self.rep), :] + self.pair_in[...].astype(F32)
        self.mine[...] = total
        self.out[...] = total.astype(BF16)
        for copy in self.scatter:
            copy.start()

    def start_gather(self):
        total = self.mine[self.rows(self.me), :]
        for s, copy in enumerate(self.scatter):
            copy.wait_recv()
            total = total + self.arrived[s].astype(F32)
        self.full[self.rep, self.rows(self.me), :] = total.astype(BF16)
        for copy in self.gather_out:
            copy.start()

    def start_share(self):
        for copy in self.gather_in:
            copy.wait_recv()
        self.share.start()

    def finish(self, result_ref):
        self.share_in.wait_recv()
        flat = self.full[...].astype(F32).reshape(2 * self.half, 128)
        for d in range(result_ref.shape[0]):
            block = flat[32 * d : 32 * d + 32]
            result_ref[d, 0:32, :] = block[:, 0:64]
            result_ref[d, 32:64, :] = block[:, 64:128]
        for copy in [self.pair, self.share] + self.scatter + self.gather_out:
            copy.wait_send()


def layers_kernel(
    owners, send_ref, nbr_ref, features_ref, up_ref, mask_ref, one_ref, two_ref, own_ref, terms_ref,
    output_ref, grad_one_ref, grad_two_ref,
    x_table, x_out, hidden_table, hidden_out, terms_in, shifted_ref, pre_ref, wide_ref, home_ref,
    bricks_ref, halo_sems, *rest
):
    bricks = own_ref.shape[0]
    slots = send_ref.shape[1]
    me, rep = lax.axis_index("space"), lax.axis_index("rep")
    barrier = pltpu.get_barrier_semaphore()
    mesh_id = pl.DeviceIdType.MESH
    for s in range(1, owners):
        there = {"space": (me + s) % owners}
        pl.semaphore_signal(barrier, inc=1, device_id=there, device_id_type=mesh_id)
    pl.semaphore_signal(barrier, inc=1, device_id={"rep": 1 - rep}, device_id_type=mesh_id)

    x_halo = Halo(owners, slots, 1, x_out, x_table, bricks, halo_sems.at[0])
    back_halo = Halo(owners, slots, -1, terms_ref, terms_in, 0, halo_sems.at[1])
    hidden_halo = Halo(owners, slots, 1, hidden_out, hidden_table, bricks, halo_sems.at[2])
    one, two = Total(owners, *rest[:8]), Total(owners, *rest[8:])

    wide_ref[...] = expand_mask(mask_ref)
    for b in range(bricks):
        part = wide_ref[:, BE * b : BE * b + BE, :]
        bricks_ref[b] = (features_ref[b].astype(F32) * part).astype(BF16)
    x_table[0:bricks] = bricks_ref[...]
    empty = jnp.zeros(x_table.shape[1:], BF16)
    x_table[x_table.shape[0] - 1] = empty
    hidden_table[x_table.shape[0] - 1] = empty
    fill_outbound(send_ref, bricks_ref, x_out, bricks)
    pl.semaphore_wait(barrier, owners)
    x_halo.start()
    back_halo.start()
    for total in (one, two):
        size = 32 * grad_one_ref.shape[0]
        total.grad[size:, :] = jnp.zeros((total.grad.shape[0] - size, 128), F32)
    x_halo.wait_recv()

    assemble(x_table, nbr_ref, shifted_ref)
    banded_conv(shifted_ref, one_ref, pre_ref)
    pre = pre_ref[...]
    hidden = wide_ref[...] * (pre * jax.nn.sigmoid(pre))
    for b in range(bricks):
        bricks_ref[b] = hidden[:, BE * b : BE * b + BE, :].astype(BF16)
    hidden_table[0:bricks] = bricks_ref[...]
    fill_outbound(send_ref, bricks_ref, hidden_out, bricks)
    hidden_halo.start()

    back_halo.wait_recv()
    home_ref[...] = own_ref[...]
    for k, (comes, unused) in enumerate(back_halo.receives):

        @pl.when(comes)
        def add_terms():
            for s in range(slots):
                term = terms_in[slots * k + s].astype(F32)
                for b in range(bricks):
                    home_ref[b] += jnp.where(send_ref[k, s] == b, term, 0.0)

    back = jnp.concatenate([home_ref[b] for b in range(bricks)], axis=1)
    pre = pre_ref[...]
    logistic = jax.nn.sigmoid(pre)
    slope = logistic * (1.0 + pre * (1.0 - logistic))
    inner = (wide_ref[...] * back * slope).astype(BF16).astype(F32)
    banded_grad(shifted_ref, inner.reshape(-1, inner.shape[2]), one.grad)
    one.start_pair()

    hidden_halo.wait_recv()
    assemble(hidden_table, nbr_ref, shifted_ref)
    one.start_scatter()
    up = (to_rows(up_ref) * wide_ref[...]).astype(BF16).astype(F32)
    banded_grad(shifted_ref, up.reshape(-1, up.shape[2]), two.grad)
    two.start_pair()
    one.start_gather()
    two.start_scatter()
    banded_conv(shifted_ref, two_ref, pre_ref)
    post = pre_ref[...] * wide_ref[...]
    for b in range(bricks):
        output_ref[b] = post[:, BE * b : BE * b + BE, :].astype(BF16)
    one.start_share()
    two.start_gather()
    one.finish(grad_one_ref)
    two.start_share()
    two.finish(grad_two_ref)
    for halo in (x_halo, back_halo, hidden_halo):
        halo.wait_send()


def banded(weight):
    split = weight.reshape(9, 3, 64, 64)
    left = jnp.pad(split, ((0, 0), (0, 1), (0, 0), (0, 0)))
    right = jnp.pad(split, ((0, 0), (1, 0), (0, 0), (0, 0)))
    return jnp.concatenate([left, right], axis=-1).reshape(9, 256, 128)


def call(body, specs, outs, scratch, args, **params):
    return pl.pallas_call(
        body,
        out_shape=outs,
        in_specs=specs,
        out_specs=[VM] * len(outs),
        scratch_shapes=scratch,
        compiler_params=pltpu.CompilerParams(vmem_limit_bytes=LIMIT, **params),
    )(*args)


def per_device(features, weight_one, weight_two, grad_out, active, send_list, local_nbr):
    bricks = features.shape[1]
    width = features.shape[4]
    brick = features.shape[2:]
    send = send_list[0, 0]
    nbr = local_nbr[0]
    owners = lax.axis_size("space")
    slots = send.shape[1]
    mask = active[0].reshape(bricks, BE, BE, BE).transpose(1, 0, 2, 3).reshape(-1, BE)
    mask = mask.astype(F32)
    kernel_one = banded(weight_one)
    kernel_two = banded(weight_two)
    kernel_back = banded(jnp.flip(weight_two, 0).transpose(0, 2, 1))

    shape = jax.ShapeDtypeStruct
    moved = send.shape[0] * slots
    bricks_half = shape((bricks,) + brick, BF16)
    bricks_full = shape((bricks,) + brick, F32)
    entries = bricks + moved + 1
    rows = bricks * BE
    own_back, terms = call(
        spread_kernel,
        [SM, VM, VM, VM],
        [bricks_full, shape((moved,) + brick, BF16)],
        [
            pltpu.VMEM((3, BE + 4, 16 * bricks, width + 256), BF16),
            pltpu.VMEM((BE + 2, 16 * bricks, width + 128), F32),
            pltpu.VMEM((entries,) + brick, F32),
        ],
        (nbr, grad_out[0], mask, kernel_back),
    )
    grads = shape(weight_one.shape, F32)
    chunk = -(-32 * weight_one.shape[0] // (2 * owners * 16)) * 16
    half = owners * chunk
    total = [
        pltpu.VMEM((2 * half, 128), F32),
        pltpu.VMEM((half, 128), BF16),
        pltpu.VMEM((half, 128), BF16),
        pltpu.VMEM((half, 128), F32),
        pltpu.VMEM((half, 128), BF16),
        pltpu.VMEM((owners - 1, chunk, 128), BF16),
        pltpu.VMEM((2, half, 128), BF16),
        pltpu.SemaphoreType.DMA((2, 2 * owners)),
    ]
    table = pltpu.VMEM((entries,) + brick, BF16)
    outgoing = pltpu.VMEM((moved,) + brick, BF16)
    output, grad_one, grad_two = call(
        functools.partial(layers_kernel, owners),
        [SM, SM] + [VM] * 7,
        [bricks_half, grads, grads],
        [
            table,
            outgoing,
            table,
            outgoing,
            outgoing,
            pltpu.VMEM((3, BE + 2, rows, width + 128), BF16),
            pltpu.VMEM((BE, rows, width), F32),
            pltpu.VMEM((BE, rows, width), F32),
            pltpu.VMEM((bricks,) + brick, F32),
            pltpu.VMEM((bricks,) + brick, BF16),
            pltpu.SemaphoreType.DMA((3, 2, send.shape[0])),
        ]
        + total
        + total,
        (send, nbr, features[0], grad_out[0], mask, kernel_one, kernel_two, own_back, terms),
        collective_id=0,
        has_side_effects=True,
    )
    return (output.reshape(features.shape), grad_one, grad_two)


def solution(mesh):
    in_specs = (
        P("rep", ("groups", "space"), None, None, None),
        P(),
        P(),
        P("rep", ("groups", "space"), None, None, None),
        P("rep", ("groups", "space"), None),
        P("rep", ("groups", "space"), None, None),
        P("rep", ("groups", "space"), None),
    )
    out_specs = (
        P("rep", ("groups", "space"), None, None, None),
        P("groups", None, None),
        P("groups", None, None),
    )
    return jax.shard_map(
        per_device, mesh=mesh, in_specs=in_specs, out_specs=out_specs, check_vma=False
    )
```

```python
import functools

import jax
import jax.numpy as jnp
from jax import lax
from jax.experimental import pallas as pl
from jax.experimental.pallas import tpu as pltpu
from jax.sharding import PartitionSpec as P

BE = 8
F32 = jnp.float32
BF16 = jnp.bfloat16
LIMIT = 48 * 1024 * 1024
VM = pl.BlockSpec(memory_space=pltpu.VMEM)
SM = pl.BlockSpec(memory_space=pltpu.SMEM)


def iota(shape, dim):
    return lax.broadcasted_iota(jnp.int32, shape, dim)


def expand_mask(mask_ref):
    rows, edge = mask_ref.shape
    width = edge * 64
    spread = (iota((edge, width), 1) // 64 == iota((edge, width), 0)).astype(BF16)
    wide = jnp.dot(mask_ref[...].astype(BF16), spread, preferred_element_type=F32)
    return wide.reshape(BE, rows // BE, width)


def to_rows(ref):
    return jnp.concatenate([ref[b].astype(F32) for b in range(ref.shape[0])], axis=1)


def pack_shell(planes):
    width = planes[0].shape[1]
    quarter, middle = iota((BE, 128), 1), width // 2
    rows, rows_short = iota((BE, width), 0), iota((BE, middle), 0)

    def gather(pairs):
        out = jnp.zeros((BE, width), F32)
        for r, (x, y) in enumerate(pairs):
            out = jnp.where(rows == r, planes[x][y : y + 1, :], out)
        return out

    ends = [
        jnp.where(quarter < 64, p[:, 0:128], p[:, width - 128 :]) for p in planes[1 : BE - 1]
    ]
    edge = [(x, y) for x in range(1, BE - 1) for y in (0, BE - 1)]
    left = gather(edge[BE:])
    spare = jnp.where(rows_short < 4, left[:, :middle], pltpu.roll(left[:, middle:], 4, 0))
    third = jnp.concatenate(ends[:4], axis=1)
    fourth = jnp.concatenate(ends[4:] + [spare], axis=1)
    return [planes[0], planes[BE - 1], third, fourth, gather(edge[:BE])]


def unpack_shell(tiles):
    width = tiles[0].shape[1]
    quarter, middle = iota((BE, 128), 1), width // 2
    rows = iota((BE, width), 0)
    spare = tiles[3][:, middle:]
    left = jnp.concatenate([spare, pltpu.roll(spare, 4, 0)], axis=1)
    ends = [tiles[2][:, 128 * q : 128 * q + 128] for q in range(4)]
    ends += [tiles[3][:, 128 * q : 128 * q + 128] for q in range(2)]
    planes = [tiles[0]]
    for q, end in enumerate(ends):
        source, r = (tiles[4], 2 * q) if q < 4 else (left, 2 * q - BE)
        low = jnp.where(quarter < 64, end, 0.0)
        high = jnp.where(quarter >= 64, end, 0.0)
        plane = jnp.concatenate([low, jnp.zeros((BE, width - 256), F32), high], axis=1)
        plane = jnp.where(rows == 0, source[r : r + 1, :], plane)
        planes.append(jnp.where(rows == BE - 1, source[r + 1 : r + 2, :], plane))
    return planes + [tiles[1]]


def pack_bricks(source_ref, base, packed_ref):
    def step(t, carry):
        tiles = pack_shell([source_ref[base + t, x].astype(F32) for x in range(BE)])
        for q, tile in enumerate(tiles):
            packed_ref[t, q] = tile.astype(BF16)
        return carry

    lax.fori_loop(0, packed_ref.shape[0], step, 0)


def unpack_arrived(halo, slots, landing_ref, table_ref, base):
    for k, (comes, copy) in enumerate(halo.receives):

        @pl.when(comes)
        def unpack():
            copy.wait_recv()

            def step(t, carry):
                tiles = [landing_ref[t, q].astype(F32) for q in range(5)]
                for x, plane in enumerate(unpack_shell(tiles)):
                    table_ref[base + t, x] = plane.astype(BF16)
                return carry

            lax.fori_loop(slots * k, slots * k + slots, step, 0)


def fill_outbound(send_ref, bricks_ref, out_ref, bricks):
    slots = send_ref.shape[1]
    for k in range(send_ref.shape[0]):
        for s in range(slots):
            out_ref[slots * k + s] = bricks_ref[jnp.minimum(send_ref[k, s], bricks - 1)]


def assemble(table_ref, nbr_ref, shifted_ref):
    width = table_ref.shape[3]
    lanes = iota((BE, 128), 1)
    rows = iota((BE, width + 128), 0)

    def plane(b, direction, source):
        strips = []
        for j in range(3):
            first = direction + 3 * j
            mid = table_ref[nbr_ref[b, first + 1], source].astype(F32)
            low = table_ref[nbr_ref[b, first], source, :, width - 128 : width].astype(F32)
            high = table_ref[nbr_ref[b, first + 2], source, :, 0:128].astype(F32)
            end = mid[:, width - 128 :]
            body = jnp.concatenate(
                [mid[:, : width - 128], jnp.where(lanes >= 64, low, end)], axis=1
            )
            tail = jnp.where(lanes < 64, high, end)
            strips.append(
                jnp.concatenate([pltpu.roll(body, 64, 1), pltpu.roll(tail, 64, 1)], axis=1)
            )
        before = pltpu.roll(jnp.where(rows == BE - 1, strips[0], strips[1]), 1, 0)
        after = pltpu.roll(jnp.where(rows == 0, strips[2], strips[1]), BE - 1, 0)
        return before, strips[1], after

    def step(x, carry):
        side = jnp.where(x == 0, 0, jnp.where(x == BE + 1, 2, 1))
        source = lax.rem(x + BE - 1, BE)
        for pair in range(nbr_ref.shape[0] // 2):
            one = plane(2 * pair, 9 * side, source)
            two = plane(2 * pair + 1, 9 * side, source)
            for j in range(3):
                both = jnp.concatenate([one[j], two[j]], axis=0).astype(BF16)
                shifted_ref[j, x, 16 * pair : 16 * pair + 16, :] = both
        return carry

    lax.fori_loop(0, BE + 2, step, 0)


def banded_conv(shifted_ref, kernel_ref, result_ref):
    length, rows, width = result_ref.shape

    def step(p, carry):
        at = pl.multiple_of(p * 128, 128)
        total = jnp.zeros((length * rows, 128), F32)
        for i in range(3):
            for j in range(3):
                block = shifted_ref[j, i : i + length, :, pl.ds(at, 256)]
                total = total + jnp.dot(
                    block.reshape(length * rows, 256),
                    kernel_ref[3 * i + j],
                    preferred_element_type=F32,
                )
        result_ref[:, :, pl.ds(at, 128)] = total.reshape(length, rows, 128)
        return carry

    lax.fori_loop(0, width // 128, step, 0)


def banded_grad(shifted_ref, upward, grad_ref):
    rows, width = upward.shape
    turned = [
        upward[:, 128 * p : 128 * p + 128].T.astype(BF16) for p in range(width // 128)
    ]

    def step(i, carry):
        for j in range(3):
            total = jnp.zeros((128, 256), F32)
            for p in range(width // 128):
                block = shifted_ref[j, pl.ds(i, BE), :, 128 * p : 128 * p + 256]
                total = total + jnp.dot(
                    turned[p], block.reshape(rows, 256), preferred_element_type=F32
                )
            flat = total.T
            for k in range(3):
                block = (
                    flat[64 * k : 64 * k + 64, 0:64] + flat[64 * k + 64 : 64 * k + 128, 64:128]
                )
                at = pl.multiple_of(32 * (9 * i + 3 * j + k), 32)
                grad_ref[pl.ds(at, 32), :] = jnp.concatenate([block[0:32], block[32:64]], axis=1)
        return carry

    lax.fori_loop(0, 3, step, 0)


def spread_kernel(nbr_ref, up_ref, mask_ref, kernel_ref, own_ref, *rest):
    out_ref, shifted_ref, spread_ref, totals_ref = rest
    bricks, width = own_ref.shape[0], own_ref.shape[3]
    wide = expand_mask(mask_ref)
    up = (to_rows(up_ref) * wide).astype(BF16).astype(F32)
    for j in range(3):
        for x in (0, 1, BE + 2, BE + 3):
            shifted_ref[j, x] = jnp.zeros(shifted_ref.shape[2:], BF16)
    for x in range(BE):
        for b in range(bricks):
            tile = up[x, BE * b : BE * b + BE, :]
            side = jnp.zeros((BE, 128), F32)
            tile = jnp.concatenate([side, tile, side], axis=1)
            tile = jnp.concatenate([tile, jnp.zeros_like(tile)], axis=0)
            for j in range(3):
                moved = pltpu.roll(tile, 2 - j, 0) if j < 2 else tile
                shifted_ref[j, x + 2, 16 * b : 16 * b + 16, :] = moved.astype(BF16)
    banded_conv(shifted_ref, kernel_ref, spread_ref)

    def clear(t, carry):
        totals_ref[t] = jnp.zeros(totals_ref.shape[1:], F32)
        return carry

    lax.fori_loop(0, totals_ref.shape[0], clear, 0)
    lanes = iota((BE, 128), 1)
    rows = iota((BE, width), 0)
    rows_short = iota((BE, 128), 0)

    def deposit(x, carry):
        side = jnp.where(x == 0, 0, jnp.where(x == BE + 1, 2, 1))
        target = lax.rem(x + BE - 1, BE)
        for b in range(bricks):
            tile = spread_ref[x, 16 * b : 16 * b + 16, :]
            tile = pltpu.roll(pltpu.roll(tile, width + 64, 1), 15, 0)
            for j in range(3):
                first = 9 * side + 3 * j
                body = tile[0:BE, 0:width] if j == 1 else tile[BE : 2 * BE, 0:width]
                ends = tile[0:BE, width:] if j == 1 else tile[BE : 2 * BE, width:]
                if j != 1:
                    keep = BE - 1 if j == 0 else 0
                    body = jnp.where(rows == keep, body, 0.0)
                    ends = jnp.where(rows_short == keep, ends, 0.0)
                totals_ref[nbr_ref[b, first + 1], target] += body
                totals_ref[nbr_ref[b, first], target, :, width - 128 : width] += jnp.where(
                    lanes >= 64, ends, 0.0
                )
                totals_ref[nbr_ref[b, first + 2], target, :, 0:128] += jnp.where(
                    lanes < 64, ends, 0.0
                )
        return carry

    lax.fori_loop(0, BE + 2, deposit, 0)
    own_ref[...] = totals_ref[0:bricks]
    pack_bricks(totals_ref, bricks, out_ref)


def remote(source, target, sems, index, device):
    return pltpu.make_async_remote_copy(
        src_ref=source,
        dst_ref=target,
        send_sem=sems.at[0, index],
        recv_sem=sems.at[1, index],
        device_id=device,
        device_id_type=pl.DeviceIdType.MESH,
    )


class Halo:
    def __init__(self, owners, slots, sign, source, target, base, sems):
        half = owners // 2
        me = lax.axis_index("space")
        row, column = me // half, me % half
        self.sends, self.receives = [], []
        steps = [(0, -1), (0, 1), (1, -1), (1, 0), (1, 1), (-1, -1), (-1, 0), (-1, 1)]
        for k, (down, right) in enumerate(steps):
            down, right = sign * down, sign * right
            to_row, to_column = row + down, column + right
            from_row, from_column = row - down, column - right
            goes = (to_row >= 0) & (to_row < 2) & (to_column >= 0) & (to_column < half)
            comes = (from_row >= 0) & (from_row < 2) & (from_column >= 0) & (from_column < half)
            device = {"space": (me + down * half + right + owners) % owners}
            copy = remote(
                source.at[slots * k : slots * k + slots],
                target.at[base + slots * k : base + slots * k + slots],
                sems,
                k,
                device,
            )
            self.sends.append((goes, copy))
            self.receives.append((comes, copy))

    def start(self):
        for goes, copy in self.sends:
            pl.when(goes)(copy.start)

    def wait_send(self):
        for goes, copy in self.sends:
            pl.when(goes)(copy.wait_send)


class Total:
    def __init__(self, owners, grad, pair_out, pair_in, mine, out, arrived, full, sems):
        self.owners = owners
        self.me = lax.axis_index("space")
        self.rep = lax.axis_index("rep")
        self.grad, self.pair_out, self.mine, self.out = grad, pair_out, mine, out
        self.pair_in, self.arrived, self.full = pair_in, arrived, full
        self.half = mine.shape[0]
        self.chunk = self.half // owners
        other = {"rep": 1 - self.rep}
        self.pair = remote(pair_out, pair_in, sems, 0, other)
        self.scatter, self.gather_out, self.gather_in = [], [], []
        own = full.at[self.rep, self.rows(self.me), :]
        for s in range(1, owners):
            there = (self.me + s) % owners
            device = {"space": there}
            self.scatter.append(
                remote(out.at[self.rows(there), :], arrived.at[s - 1], sems, s, device)
            )
            landing = full.at[self.rep, self.rows((self.me + owners - s) % owners), :]
            index = owners + s
            self.gather_out.append(remote(own, own, sems, index, device))
            self.gather_in.append(remote(landing, landing, sems, index, device))
        self.share = remote(full.at[self.rep], full.at[self.rep], sems, owners, other)
        coming = full.at[1 - self.rep]
        self.share_in = remote(coming, coming, sems, owners, other)

    def rows(self, owner):
        return pl.ds(pl.multiple_of(owner * self.chunk, self.chunk), self.chunk)

    def halves(self, rep):
        return pl.ds(pl.multiple_of(rep * self.half, self.half), self.half)

    def start_pair(self):
        self.pair_out[...] = self.grad[self.halves(1 - self.rep), :].astype(BF16)
        self.pair.start()

    def start_scatter(self):
        self.pair.wait_recv()
        total = self.grad[self.halves(self.rep), :] + self.pair_in[...].astype(F32)
        self.mine[...] = total
        self.out[...] = total.astype(BF16)
        for copy in self.scatter:
            copy.start()

    def start_gather(self):
        total = self.mine[self.rows(self.me), :]
        for s, copy in enumerate(self.scatter):
            copy.wait_recv()
            total = total + self.arrived[s].astype(F32)
        self.full[self.rep, self.rows(self.me), :] = total.astype(BF16)
        for copy in self.gather_out:
            copy.start()

    def start_share(self):
        for copy in self.gather_in:
            copy.wait_recv()
        self.share.start()

    def finish(self, result_ref):
        self.share_in.wait_recv()
        flat = self.full[...].astype(F32).reshape(2 * self.half, 128)
        for d in range(result_ref.shape[0]):
            block = flat[32 * d : 32 * d + 32]
            result_ref[d, 0:32, :] = block[:, 0:64]
            result_ref[d, 32:64, :] = block[:, 64:128]
        for copy in [self.pair, self.share] + self.scatter + self.gather_out:
            copy.wait_send()


def layers_kernel(
    owners, send_ref, nbr_ref, features_ref, up_ref, mask_ref, one_ref, two_ref, own_ref, terms_ref,
    output_ref, grad_one_ref, grad_two_ref,
    table_ref, x_out, x_in, hidden_out, hidden_in, terms_in, packed_ref, shifted_ref, pre_ref, wide_ref, home_ref,
    bricks_ref, halo_sems, *rest
):
    bricks = own_ref.shape[0]
    slots = send_ref.shape[1]
    me, rep = lax.axis_index("space"), lax.axis_index("rep")
    barrier = pltpu.get_barrier_semaphore()
    mesh_id = pl.DeviceIdType.MESH
    for s in range(1, owners):
        there = {"space": (me + s) % owners}
        pl.semaphore_signal(barrier, inc=1, device_id=there, device_id_type=mesh_id)
    pl.semaphore_signal(barrier, inc=1, device_id={"rep": 1 - rep}, device_id_type=mesh_id)

    x_halo = Halo(owners, slots, 1, x_out, x_in, 0, halo_sems.at[0])
    back_halo = Halo(owners, slots, -1, terms_ref, terms_in, 0, halo_sems.at[1])
    hidden_halo = Halo(owners, slots, 1, hidden_out, hidden_in, 0, halo_sems.at[2])
    one, two = Total(owners, *rest[:8]), Total(owners, *rest[8:])

    wide_ref[...] = expand_mask(mask_ref)
    for b in range(bricks):
        part = wide_ref[:, BE * b : BE * b + BE, :]
        bricks_ref[b] = (features_ref[b].astype(F32) * part).astype(BF16)
    table_ref[0:bricks] = bricks_ref[...]
    table_ref[table_ref.shape[0] - 1] = jnp.zeros(table_ref.shape[1:], BF16)
    pack_bricks(bricks_ref, 0, packed_ref)
    fill_outbound(send_ref, packed_ref, x_out, bricks)
    pl.semaphore_wait(barrier, owners)
    x_halo.start()
    back_halo.start()
    for total in (one, two):
        size = 32 * grad_one_ref.shape[0]
        total.grad[size:, :] = jnp.zeros((total.grad.shape[0] - size, 128), F32)
    unpack_arrived(x_halo, slots, x_in, table_ref, bricks)

    assemble(table_ref, nbr_ref, shifted_ref)
    banded_conv(shifted_ref, one_ref, pre_ref)
    pre = pre_ref[...]
    hidden = wide_ref[...] * (pre * jax.nn.sigmoid(pre))
    for b in range(bricks):
        bricks_ref[b] = hidden[:, BE * b : BE * b + BE, :].astype(BF16)
    pack_bricks(bricks_ref, 0, packed_ref)
    fill_outbound(send_ref, packed_ref, hidden_out, bricks)
    hidden_halo.start()
    table_ref[0:bricks] = bricks_ref[...]

    home_ref[...] = own_ref[...]
    for k, (comes, copy) in enumerate(back_halo.receives):

        @pl.when(comes)
        def add_terms():
            copy.wait_recv()

            def step(s, carry):
                tiles = [terms_in[slots * k + s, q].astype(F32) for q in range(5)]
                for x, plane in enumerate(unpack_shell(tiles)):
                    for b in range(bricks):
                        home_ref[b, x] += jnp.where(send_ref[k, s] == b, plane, 0.0)
                return carry

            lax.fori_loop(0, slots, step, 0)

    back = jnp.concatenate([home_ref[b] for b in range(bricks)], axis=1)
    pre = pre_ref[...]
    logistic = jax.nn.sigmoid(pre)
    slope = logistic * (1.0 + pre * (1.0 - logistic))
    inner = (wide_ref[...] * back * slope).astype(BF16).astype(F32)
    banded_grad(shifted_ref, inner.reshape(-1, inner.shape[2]), one.grad)
    one.start_pair()

    unpack_arrived(hidden_halo, slots, hidden_in, table_ref, bricks)
    assemble(table_ref, nbr_ref, shifted_ref)
    one.start_scatter()
    up = (to_rows(up_ref) * wide_ref[...]).astype(BF16).astype(F32)
    banded_grad(shifted_ref, up.reshape(-1, up.shape[2]), two.grad)
    two.start_pair()
    one.start_gather()
    two.start_scatter()
    banded_conv(shifted_ref, two_ref, pre_ref)
    post = pre_ref[...] * wide_ref[...]
    for b in range(bricks):
        output_ref[b] = post[:, BE * b : BE * b + BE, :].astype(BF16)
    one.start_share()
    two.start_gather()
    one.finish(grad_one_ref)
    two.start_share()
    two.finish(grad_two_ref)
    for halo in (x_halo, back_halo, hidden_halo):
        halo.wait_send()


def banded(weight):
    split = weight.reshape(9, 3, 64, 64)
    left = jnp.pad(split, ((0, 0), (0, 1), (0, 0), (0, 0)))
    right = jnp.pad(split, ((0, 0), (1, 0), (0, 0), (0, 0)))
    return jnp.concatenate([left, right], axis=-1).reshape(9, 256, 128)


def call(body, specs, outs, scratch, args, **params):
    return pl.pallas_call(
        body,
        out_shape=outs,
        in_specs=specs,
        out_specs=[VM] * len(outs),
        scratch_shapes=scratch,
        compiler_params=pltpu.CompilerParams(vmem_limit_bytes=LIMIT, **params),
    )(*args)


def per_device(features, weight_one, weight_two, grad_out, active, send_list, local_nbr):
    bricks = features.shape[1]
    width = features.shape[4]
    brick = features.shape[2:]
    send = send_list[0, 0]
    nbr = local_nbr[0]
    owners = lax.axis_size("space")
    slots = send.shape[1]
    mask = active[0].reshape(bricks, BE, BE, BE).transpose(1, 0, 2, 3).reshape(-1, BE)
    mask = mask.astype(F32)
    kernel_one = banded(weight_one)
    kernel_two = banded(weight_two)
    kernel_back = banded(jnp.flip(weight_two, 0).transpose(0, 2, 1))

    shape = jax.ShapeDtypeStruct
    moved = send.shape[0] * slots
    shell = (5, BE, width)
    bricks_half = shape((bricks,) + brick, BF16)
    bricks_full = shape((bricks,) + brick, F32)
    entries = bricks + moved + 1
    rows = bricks * BE
    own_back, terms = call(
        spread_kernel,
        [SM, VM, VM, VM],
        [bricks_full, shape((moved,) + shell, BF16)],
        [
            pltpu.VMEM((3, BE + 4, 16 * bricks, width + 256), BF16),
            pltpu.VMEM((BE + 2, 16 * bricks, width + 128), F32),
            pltpu.VMEM((entries,) + brick, F32),
        ],
        (nbr, grad_out[0], mask, kernel_back),
    )
    grads = shape(weight_one.shape, F32)
    chunk = -(-32 * weight_one.shape[0] // (2 * owners * 16)) * 16
    half = owners * chunk
    total = [
        pltpu.VMEM((2 * half, 128), F32),
        pltpu.VMEM((half, 128), BF16),
        pltpu.VMEM((half, 128), BF16),
        pltpu.VMEM((half, 128), F32),
        pltpu.VMEM((half, 128), BF16),
        pltpu.VMEM((owners - 1, chunk, 128), BF16),
        pltpu.VMEM((2, half, 128), BF16),
        pltpu.SemaphoreType.DMA((2, 2 * owners)),
    ]
    table = pltpu.VMEM((entries,) + brick, BF16)
    moving = pltpu.VMEM((moved,) + shell, BF16)
    output, grad_one, grad_two = call(
        functools.partial(layers_kernel, owners),
        [SM, SM] + [VM] * 7,
        [bricks_half, grads, grads],
        [
            table,
            moving,
            moving,
            moving,
            moving,
            moving,
            pltpu.VMEM((bricks,) + shell, BF16),
            pltpu.VMEM((3, BE + 2, rows, width + 128), BF16),
            pltpu.VMEM((BE, rows, width), F32),
            pltpu.VMEM((BE, rows, width), F32),
            pltpu.VMEM((bricks,) + brick, F32),
            pltpu.VMEM((bricks,) + brick, BF16),
            pltpu.SemaphoreType.DMA((3, 2, send.shape[0])),
        ]
        + total
        + total,
        (send, nbr, features[0], grad_out[0], mask, kernel_one, kernel_two, own_back, terms),
        collective_id=0,
        has_side_effects=True,
    )
    return (output.reshape(features.shape), grad_one, grad_two)


def solution(mesh):
    in_specs = (
        P("rep", ("groups", "space"), None, None, None),
        P(),
        P(),
        P("rep", ("groups", "space"), None, None, None),
        P("rep", ("groups", "space"), None),
        P("rep", ("groups", "space"), None, None),
        P("rep", ("groups", "space"), None),
    )
    out_specs = (
        P("rep", ("groups", "space"), None, None, None),
        P("groups", None, None),
        P("groups", None, None),
    )
    return jax.shard_map(
        per_device, mesh=mesh, in_specs=in_specs, out_specs=out_specs, check_vma=False
    )
```

```python
import functools

import jax
import jax.numpy as jnp
from jax import lax
from jax.experimental import pallas as pl
from jax.experimental.pallas import tpu as pltpu
from jax.sharding import PartitionSpec as P

BE = 8
F32 = jnp.float32
BF16 = jnp.bfloat16
LIMIT = 48 * 1024 * 1024
VM = pl.BlockSpec(memory_space=pltpu.VMEM)
SM = pl.BlockSpec(memory_space=pltpu.SMEM)


def iota(shape, dim):
    return lax.broadcasted_iota(jnp.int32, shape, dim)


def expand_mask(mask_ref):
    rows, edge = mask_ref.shape
    width = edge * 64
    spread = (iota((edge, width), 1) // 64 == iota((edge, width), 0)).astype(BF16)
    wide = jnp.dot(mask_ref[...].astype(F32).astype(BF16), spread, preferred_element_type=F32)
    return wide.reshape(BE, rows // BE, width)


def to_rows(ref):
    return jnp.concatenate([ref[b].astype(F32) for b in range(ref.shape[0])], axis=1)


def pack_shell(planes):
    width = planes[0].shape[1]
    quarter, middle = iota((BE, 128), 1), width // 2
    rows, rows_short = iota((BE, width), 0), iota((BE, middle), 0)

    def gather(pairs):
        out = jnp.zeros((BE, width), F32)
        for r, (x, y) in enumerate(pairs):
            out = jnp.where(rows == r, planes[x][y : y + 1, :], out)
        return out

    ends = [
        jnp.where(quarter < 64, p[:, 0:128], p[:, width - 128 :]) for p in planes[1 : BE - 1]
    ]
    edge = [(x, y) for x in range(1, BE - 1) for y in (0, BE - 1)]
    left = gather(edge[BE:])
    spare = jnp.where(rows_short < 4, left[:, :middle], pltpu.roll(left[:, middle:], 4, 0))
    third = jnp.concatenate(ends[:4], axis=1)
    fourth = jnp.concatenate(ends[4:] + [spare], axis=1)
    return [planes[0], planes[BE - 1], third, fourth, gather(edge[:BE])]


def unpack_shell(tiles):
    width = tiles[0].shape[1]
    quarter, middle = iota((BE, 128), 1), width // 2
    rows = iota((BE, width), 0)
    spare = tiles[3][:, middle:]
    left = jnp.concatenate([spare, pltpu.roll(spare, 4, 0)], axis=1)
    ends = [tiles[2][:, 128 * q : 128 * q + 128] for q in range(4)]
    ends += [tiles[3][:, 128 * q : 128 * q + 128] for q in range(2)]
    planes = [tiles[0]]
    for q, end in enumerate(ends):
        source, r = (tiles[4], 2 * q) if q < 4 else (left, 2 * q - BE)
        low = jnp.where(quarter < 64, end, 0.0)
        high = jnp.where(quarter >= 64, end, 0.0)
        plane = jnp.concatenate([low, jnp.zeros((BE, width - 256), F32), high], axis=1)
        plane = jnp.where(rows == 0, source[r : r + 1, :], plane)
        planes.append(jnp.where(rows == BE - 1, source[r + 1 : r + 2, :], plane))
    return planes + [tiles[1]]


def pack_bricks(source_ref, base, packed_ref):
    def step(t, carry):
        tiles = pack_shell([source_ref[base + t, x].astype(F32) for x in range(BE)])
        for q, tile in enumerate(tiles):
            packed_ref[t, q] = tile.astype(BF16)
        return carry

    lax.fori_loop(0, packed_ref.shape[0], step, 0)


def unpack_arrived(halo, slots, landing_ref, table_ref, base):
    for k, (comes, copy) in enumerate(halo.receives):

        @pl.when(comes)
        def unpack():
            copy.wait_recv()

            def step(t, carry):
                tiles = [landing_ref[t, q].astype(F32) for q in range(5)]
                for x, plane in enumerate(unpack_shell(tiles)):
                    table_ref[base + t, x] = plane.astype(BF16)
                return carry

            lax.fori_loop(slots * k, slots * k + slots, step, 0)


def fill_outbound(send_ref, bricks_ref, out_ref, bricks):
    slots = send_ref.shape[1]
    for k in range(send_ref.shape[0]):
        for s in range(slots):
            out_ref[slots * k + s] = bricks_ref[jnp.minimum(send_ref[k, s], bricks - 1)]


def assemble(table_ref, nbr_ref, shifted_ref):
    width = table_ref.shape[3]
    lanes = iota((BE, 128), 1)
    rows = iota((BE, width + 128), 0)

    def plane(b, direction, source):
        strips = []
        for j in range(3):
            first = direction + 3 * j
            mid = table_ref[nbr_ref[b, first + 1], source].astype(F32)
            low = table_ref[nbr_ref[b, first], source, :, width - 128 : width].astype(F32)
            high = table_ref[nbr_ref[b, first + 2], source, :, 0:128].astype(F32)
            end = mid[:, width - 128 :]
            body = jnp.concatenate(
                [mid[:, : width - 128], jnp.where(lanes >= 64, low, end)], axis=1
            )
            tail = jnp.where(lanes < 64, high, end)
            strips.append(
                jnp.concatenate([pltpu.roll(body, 64, 1), pltpu.roll(tail, 64, 1)], axis=1)
            )
        before = pltpu.roll(jnp.where(rows == BE - 1, strips[0], strips[1]), 1, 0)
        after = pltpu.roll(jnp.where(rows == 0, strips[2], strips[1]), BE - 1, 0)
        return before, strips[1], after

    def step(x, carry):
        side = jnp.where(x == 0, 0, jnp.where(x == BE + 1, 2, 1))
        source = lax.rem(x + BE - 1, BE)
        for pair in range(nbr_ref.shape[0] // 2):
            one = plane(2 * pair, 9 * side, source)
            two = plane(2 * pair + 1, 9 * side, source)
            for j in range(3):
                both = jnp.concatenate([one[j], two[j]], axis=0).astype(BF16)
                shifted_ref[j, x, 16 * pair : 16 * pair + 16, :] = both
        return carry

    lax.fori_loop(0, BE + 2, step, 0)


def band_forward(weight_ref, kernel_ref):
    empty = jnp.zeros((64, 64), F32)
    for n in range(9):
        three = [weight_ref[3 * n + k].astype(F32) for k in range(3)]
        left = jnp.concatenate(three + [empty], axis=0)
        right = jnp.concatenate([empty] + three, axis=0)
        kernel_ref[n] = jnp.concatenate([left, right], axis=1).astype(BF16)


def band_backward(weight_ref, kernel_ref):
    empty = jnp.zeros((64, 64), F32)
    for n in range(9):
        three = [weight_ref[26 - 3 * n - k].astype(F32) for k in range(3)]
        top = jnp.concatenate(three + [empty], axis=1)
        low = jnp.concatenate([empty] + three, axis=1)
        kernel_ref[n] = jnp.concatenate([top, low], axis=0).astype(BF16)


def banded_conv(shifted_ref, kernel_ref, result_ref, first=0, last=None, turned=False):
    length, rows, width = result_ref.shape

    def step(p, carry):
        at = pl.multiple_of(p * 128, 128)
        total = jnp.zeros((length * rows, 128), F32)
        for i in range(3):
            for j in range(3):
                block = shifted_ref[j, i : i + length, :, pl.ds(at, 256)]
                total = total + lax.dot_general(
                    block.reshape(length * rows, 256),
                    kernel_ref[3 * i + j],
                    (((1,), (1 if turned else 0,)), ((), ())),
                    preferred_element_type=F32,
                )
        result_ref[:, :, pl.ds(at, 128)] = total.reshape(length, rows, 128)
        return carry

    lax.fori_loop(first, width // 128 if last is None else last, step, 0)


def banded_grad(shifted_ref, upward, grad_ref):
    rows, width = upward.shape
    turned = [
        upward[:, 128 * p : 128 * p + 128].T.astype(BF16) for p in range(width // 128)
    ]

    def step(i, carry):
        for j in range(3):
            total = jnp.zeros((128, 256), F32)
            for p in range(width // 128):
                block = shifted_ref[j, pl.ds(i, BE), :, 128 * p : 128 * p + 256]
                total = total + jnp.dot(
                    turned[p], block.reshape(rows, 256), preferred_element_type=F32
                )
            flat = total.T
            for k in range(3):
                block = (
                    flat[64 * k : 64 * k + 64, 0:64] + flat[64 * k + 64 : 64 * k + 128, 64:128]
                )
                at = pl.multiple_of(32 * (9 * i + 3 * j + k), 32)
                grad_ref[pl.ds(at, 32), :] = jnp.concatenate([block[0:32], block[32:64]], axis=1)
        return carry

    lax.fori_loop(0, 3, step, 0)


def spread_kernel(nbr_ref, up_ref, mask_ref, weight_ref, own_ref, *rest):
    out_ref, shifted_ref, spread_ref, totals_ref, kernel_ref = rest
    band_backward(weight_ref, kernel_ref)
    bricks, width = own_ref.shape[0], own_ref.shape[3]
    wide = expand_mask(mask_ref)
    up = (to_rows(up_ref) * wide).astype(BF16).astype(F32)
    for j in range(3):
        for x in (0, 1, BE + 2, BE + 3):
            shifted_ref[j, x] = jnp.zeros(shifted_ref.shape[2:], BF16)
    for x in range(BE):
        for b in range(bricks):
            tile = up[x, BE * b : BE * b + BE, :]
            side = jnp.zeros((BE, 128), F32)
            tile = jnp.concatenate([side, tile, side], axis=1)
            tile = jnp.concatenate([tile, jnp.zeros_like(tile)], axis=0)
            for j in range(3):
                moved = pltpu.roll(tile, 2 - j, 0) if j < 2 else tile
                shifted_ref[j, x + 2, 16 * b : 16 * b + 16, :] = moved.astype(BF16)
    banded_conv(shifted_ref, kernel_ref, spread_ref, turned=True)

    def clear(t, carry):
        totals_ref[t] = jnp.zeros(totals_ref.shape[1:], F32)
        return carry

    lax.fori_loop(0, totals_ref.shape[0], clear, 0)
    lanes = iota((BE, 128), 1)
    rows = iota((BE, width), 0)
    rows_short = iota((BE, 128), 0)

    def deposit(x, carry):
        side = jnp.where(x == 0, 0, jnp.where(x == BE + 1, 2, 1))
        target = lax.rem(x + BE - 1, BE)
        for b in range(bricks):
            tile = spread_ref[x, 16 * b : 16 * b + 16, :]
            tile = pltpu.roll(pltpu.roll(tile, width + 64, 1), 15, 0)
            for j in range(3):
                first = 9 * side + 3 * j
                body = tile[0:BE, 0:width] if j == 1 else tile[BE : 2 * BE, 0:width]
                ends = tile[0:BE, width:] if j == 1 else tile[BE : 2 * BE, width:]
                if j != 1:
                    keep = BE - 1 if j == 0 else 0
                    body = jnp.where(rows == keep, body, 0.0)
                    ends = jnp.where(rows_short == keep, ends, 0.0)
                totals_ref[nbr_ref[b, first + 1], target] += body
                totals_ref[nbr_ref[b, first], target, :, width - 128 : width] += jnp.where(
                    lanes >= 64, ends, 0.0
                )
                totals_ref[nbr_ref[b, first + 2], target, :, 0:128] += jnp.where(
                    lanes < 64, ends, 0.0
                )
        return carry

    lax.fori_loop(0, BE + 2, deposit, 0)
    own_ref[...] = totals_ref[0:bricks]
    pack_bricks(totals_ref, bricks, out_ref)


def remote(source, target, sems, index, device):
    return pltpu.make_async_remote_copy(
        src_ref=source,
        dst_ref=target,
        send_sem=sems.at[0, index],
        recv_sem=sems.at[1, index],
        device_id=device,
        device_id_type=pl.DeviceIdType.MESH,
    )


class Halo:
    def __init__(self, owners, slots, sign, source, target, base, sems):
        half = owners // 2
        me = lax.axis_index("space")
        row, column = me // half, me % half
        self.sends, self.receives = [], []
        steps = [(0, -1), (0, 1), (1, -1), (1, 0), (1, 1), (-1, -1), (-1, 0), (-1, 1)]
        for k, (down, right) in enumerate(steps):
            down, right = sign * down, sign * right
            to_row, to_column = row + down, column + right
            from_row, from_column = row - down, column - right
            goes = (to_row >= 0) & (to_row < 2) & (to_column >= 0) & (to_column < half)
            comes = (from_row >= 0) & (from_row < 2) & (from_column >= 0) & (from_column < half)
            device = {"space": (me + down * half + right + owners) % owners}
            copy = remote(
                source.at[slots * k : slots * k + slots],
                target.at[base + slots * k : base + slots * k + slots],
                sems,
                k,
                device,
            )
            self.sends.append((goes, copy))
            self.receives.append((comes, copy))

    def start(self):
        for goes, copy in self.sends:
            pl.when(goes)(copy.start)

    def wait_send(self):
        for goes, copy in self.sends:
            pl.when(goes)(copy.wait_send)


class Total:
    def __init__(self, owners, grad, pair_out, pair_in, mine, out, arrived, full, sems):
        self.owners = owners
        self.me = lax.axis_index("space")
        self.rep = lax.axis_index("rep")
        self.grad, self.pair_out, self.mine, self.out = grad, pair_out, mine, out
        self.pair_in, self.arrived, self.full = pair_in, arrived, full
        self.half = mine.shape[0]
        self.chunk = self.half // owners
        other = {"rep": 1 - self.rep}
        self.pair = remote(pair_out, pair_in, sems, 0, other)
        self.scatter, self.gather_out, self.gather_in = [], [], []
        own = full.at[self.rep, self.rows(self.me), :]
        for s in range(1, owners):
            there = (self.me + s) % owners
            device = {"space": there}
            self.scatter.append(
                remote(out.at[self.rows(there), :], arrived.at[s - 1], sems, s, device)
            )
            landing = full.at[self.rep, self.rows((self.me + owners - s) % owners), :]
            index = owners + s
            self.gather_out.append(remote(own, own, sems, index, device))
            self.gather_in.append(remote(landing, landing, sems, index, device))
        self.share = remote(full.at[self.rep], full.at[self.rep], sems, owners, other)
        coming = full.at[1 - self.rep]
        self.share_in = remote(coming, coming, sems, owners, other)

    def rows(self, owner):
        return pl.ds(pl.multiple_of(owner * self.chunk, self.chunk), self.chunk)

    def halves(self, rep):
        return pl.ds(pl.multiple_of(rep * self.half, self.half), self.half)

    def start_pair(self):
        self.pair_out[...] = self.grad[self.halves(1 - self.rep), :].astype(BF16)
        self.pair.start()

    def start_scatter(self):
        self.pair.wait_recv()
        total = self.grad[self.halves(self.rep), :] + self.pair_in[...].astype(F32)
        self.mine[...] = total
        self.out[...] = total.astype(BF16)
        for copy in self.scatter:
            copy.start()

    def start_gather(self):
        total = self.mine[self.rows(self.me), :]
        for s, copy in enumerate(self.scatter):
            copy.wait_recv()
            total = total + self.arrived[s].astype(F32)
        self.full[self.rep, self.rows(self.me), :] = total.astype(BF16)
        for copy in self.gather_out:
            copy.start()

    def start_share(self):
        for copy in self.gather_in:
            copy.wait_recv()
        self.share.start()

    def finish(self, result_ref):
        self.share_in.wait_recv()
        flat = self.full[...].astype(F32).reshape(2 * self.half, 128)
        for d in range(result_ref.shape[0]):
            block = flat[32 * d : 32 * d + 32]
            result_ref[d, 0:32, :] = block[:, 0:64]
            result_ref[d, 32:64, :] = block[:, 64:128]
        for copy in [self.pair, self.share] + self.scatter + self.gather_out:
            copy.wait_send()


def layers_kernel(
    owners, send_ref, nbr_ref, features_ref, up_ref, mask_ref, one_ref, two_ref, own_ref, terms_ref,
    output_ref, grad_one_ref, grad_two_ref,
    table_ref, x_out, x_in, hidden_out, hidden_in, terms_in, packed_ref, shifted_ref, pre_ref, wide_ref, home_ref,
    bricks_ref, kernel_ref, halo_sems, *rest
):
    bricks = own_ref.shape[0]
    slots = send_ref.shape[1]
    me, rep = lax.axis_index("space"), lax.axis_index("rep")
    barrier = pltpu.get_barrier_semaphore()
    mesh_id = pl.DeviceIdType.MESH
    for s in range(1, owners):
        there = {"space": (me + s) % owners}
        pl.semaphore_signal(barrier, inc=1, device_id=there, device_id_type=mesh_id)
    pl.semaphore_signal(barrier, inc=1, device_id={"rep": 1 - rep}, device_id_type=mesh_id)

    x_halo = Halo(owners, slots, 1, x_out, x_in, 0, halo_sems.at[0])
    back_halo = Halo(owners, slots, -1, terms_ref, terms_in, 0, halo_sems.at[1])
    hidden_halo = Halo(owners, slots, 1, hidden_out, hidden_in, 0, halo_sems.at[2])
    one, two = Total(owners, *rest[:8]), Total(owners, *rest[8:])

    wide_ref[...] = expand_mask(mask_ref)
    for b in range(bricks):
        part = wide_ref[:, BE * b : BE * b + BE, :]
        bricks_ref[b] = (features_ref[b].astype(F32) * part).astype(BF16)
    table_ref[0:bricks] = bricks_ref[...]
    table_ref[table_ref.shape[0] - 1] = jnp.zeros(table_ref.shape[1:], BF16)
    pack_bricks(bricks_ref, 0, packed_ref)
    fill_outbound(send_ref, packed_ref, x_out, bricks)
    pl.semaphore_wait(barrier, owners)
    x_halo.start()
    back_halo.start()
    for total in (one, two):
        size = 32 * grad_one_ref.shape[0]
        total.grad[size:, :] = jnp.zeros((total.grad.shape[0] - size, 128), F32)
    band_forward(one_ref, kernel_ref.at[0])
    band_forward(two_ref, kernel_ref.at[1])
    unpack_arrived(x_halo, slots, x_in, table_ref, bricks)

    assemble(table_ref, nbr_ref, shifted_ref)
    banded_conv(shifted_ref, kernel_ref.at[0], pre_ref)
    pre = pre_ref[...]
    hidden = wide_ref[...] * (pre * jax.nn.sigmoid(pre))
    for b in range(bricks):
        bricks_ref[b] = hidden[:, BE * b : BE * b + BE, :].astype(BF16)
    pack_bricks(bricks_ref, 0, packed_ref)
    fill_outbound(send_ref, packed_ref, hidden_out, bricks)
    hidden_halo.start()
    table_ref[0:bricks] = bricks_ref[...]

    home_ref[...] = own_ref[...]
    for k, (comes, copy) in enumerate(back_halo.receives):

        @pl.when(comes)
        def add_terms():
            copy.wait_recv()

            def step(s, carry):
                tiles = [terms_in[slots * k + s, q].astype(F32) for q in range(5)]
                for x, plane in enumerate(unpack_shell(tiles)):
                    for b in range(bricks):
                        home_ref[b, x] += jnp.where(send_ref[k, s] == b, plane, 0.0)
                return carry

            lax.fori_loop(0, slots, step, 0)

    back = jnp.concatenate([home_ref[b] for b in range(bricks)], axis=1)
    pre = pre_ref[...]
    logistic = jax.nn.sigmoid(pre)
    slope = logistic * (1.0 + pre * (1.0 - logistic))
    inner = (wide_ref[...] * back * slope).astype(BF16).astype(F32)
    banded_grad(shifted_ref, inner.reshape(-1, inner.shape[2]), one.grad)
    one.start_pair()

    unpack_arrived(hidden_halo, slots, hidden_in, table_ref, bricks)
    assemble(table_ref, nbr_ref, shifted_ref)
    one.start_scatter()
    up = (to_rows(up_ref) * wide_ref[...]).astype(BF16).astype(F32)
    banded_grad(shifted_ref, up.reshape(-1, up.shape[2]), two.grad)
    two.start_pair()
    one.start_gather()
    banded_conv(shifted_ref, kernel_ref.at[1], pre_ref, 0, 1)
    two.start_scatter()
    banded_conv(shifted_ref, kernel_ref.at[1], pre_ref, 1, 3)
    one.start_share()
    two.start_gather()
    banded_conv(shifted_ref, kernel_ref.at[1], pre_ref, 3, 4)
    post = pre_ref[...] * wide_ref[...]
    for b in range(bricks):
        output_ref[b] = post[:, BE * b : BE * b + BE, :].astype(BF16)
    one.finish(grad_one_ref)
    two.start_share()
    two.finish(grad_two_ref)
    for halo in (x_halo, back_halo, hidden_halo):
        halo.wait_send()


def call(body, specs, outs, scratch, args, **params):
    return pl.pallas_call(
        body,
        out_shape=outs,
        in_specs=specs,
        out_specs=[VM] * len(outs),
        scratch_shapes=scratch,
        compiler_params=pltpu.CompilerParams(vmem_limit_bytes=LIMIT, **params),
    )(*args)


def per_device(features, weight_one, weight_two, grad_out, active, send_list, local_nbr):
    bricks = features.shape[1]
    width = features.shape[4]
    brick = features.shape[2:]
    send = send_list[0, 0]
    nbr = local_nbr[0]
    owners = lax.axis_size("space")
    slots = send.shape[1]
    mask = active[0].reshape(bricks, BE, BE, BE).transpose(1, 0, 2, 3).reshape(-1, BE)
    shape = jax.ShapeDtypeStruct
    moved = send.shape[0] * slots
    shell = (5, BE, width)
    bricks_half = shape((bricks,) + brick, BF16)
    bricks_full = shape((bricks,) + brick, F32)
    entries = bricks + moved + 1
    rows = bricks * BE
    own_back, terms = call(
        spread_kernel,
        [SM, VM, VM, VM],
        [bricks_full, shape((moved,) + shell, BF16)],
        [
            pltpu.VMEM((3, BE + 4, 16 * bricks, width + 256), BF16),
            pltpu.VMEM((BE + 2, 16 * bricks, width + 128), F32),
            pltpu.VMEM((entries,) + brick, F32),
            pltpu.VMEM((9, 128, 256), BF16),
        ],
        (nbr, grad_out[0], mask, weight_two),
    )
    grads = shape(weight_one.shape, F32)
    chunk = -(-32 * weight_one.shape[0] // (2 * owners * 16)) * 16
    half = owners * chunk
    total = [
        pltpu.VMEM((2 * half, 128), F32),
        pltpu.VMEM((half, 128), BF16),
        pltpu.VMEM((half, 128), BF16),
        pltpu.VMEM((half, 128), F32),
        pltpu.VMEM((half, 128), BF16),
        pltpu.VMEM((owners - 1, chunk, 128), BF16),
        pltpu.VMEM((2, half, 128), BF16),
        pltpu.SemaphoreType.DMA((2, 2 * owners)),
    ]
    table = pltpu.VMEM((entries,) + brick, BF16)
    moving = pltpu.VMEM((moved,) + shell, BF16)
    output, grad_one, grad_two = call(
        functools.partial(layers_kernel, owners),
        [SM, SM] + [VM] * 7,
        [bricks_half, grads, grads],
        [
            table,
            moving,
            moving,
            moving,
            moving,
            moving,
            pltpu.VMEM((bricks,) + shell, BF16),
            pltpu.VMEM((3, BE + 2, rows, width + 128), BF16),
            pltpu.VMEM((BE, rows, width), F32),
            pltpu.VMEM((BE, rows, width), F32),
            pltpu.VMEM((bricks,) + brick, F32),
            pltpu.VMEM((bricks,) + brick, BF16),
            pltpu.VMEM((2, 9, 256, 128), BF16),
            pltpu.SemaphoreType.DMA((3, 2, send.shape[0])),
        ]
        + total
        + total,
        (send, nbr, features[0], grad_out[0], mask, weight_one, weight_two, own_back, terms),
        collective_id=0,
        has_side_effects=True,
    )
    return (output.reshape(features.shape), grad_one, grad_two)


def solution(mesh):
    in_specs = (
        P("rep", ("groups", "space"), None, None, None),
        P(),
        P(),
        P("rep", ("groups", "space"), None, None, None),
        P("rep", ("groups", "space"), None),
        P("rep", ("groups", "space"), None, None),
        P("rep", ("groups", "space"), None),
    )
    out_specs = (
        P("rep", ("groups", "space"), None, None, None),
        P("groups", None, None),
        P("groups", None, None),
    )
    return jax.shard_map(
        per_device, mesh=mesh, in_specs=in_specs, out_specs=out_specs, check_vma=False
    )
```

```python
import functools

import jax
import jax.numpy as jnp
from jax import lax
from jax.experimental import pallas as pl
from jax.experimental.pallas import tpu as pltpu
from jax.sharding import PartitionSpec as P

BE = 8
F32 = jnp.float32
BF16 = jnp.bfloat16
LIMIT = 48 * 1024 * 1024
VM = pl.BlockSpec(memory_space=pltpu.VMEM)
SM = pl.BlockSpec(memory_space=pltpu.SMEM)


def iota(shape, dim):
    return lax.broadcasted_iota(jnp.int32, shape, dim)


def expand_mask(mask_ref):
    rows, edge = mask_ref.shape
    width = edge * 64
    spread = (iota((edge, width), 1) // 64 == iota((edge, width), 0)).astype(BF16)
    wide = jnp.dot(mask_ref[...].astype(F32).astype(BF16), spread, preferred_element_type=F32)
    return wide.reshape(BE, rows // BE, width)


def to_rows(ref):
    return jnp.concatenate([ref[b].astype(F32) for b in range(ref.shape[0])], axis=1)


def pack_shell(planes):
    width = planes[0].shape[1]
    quarter, middle = iota((BE, 128), 1), width // 2
    rows, rows_short = iota((BE, width), 0), iota((BE, middle), 0)

    def gather(pairs):
        out = jnp.zeros((BE, width), F32)
        for r, (x, y) in enumerate(pairs):
            out = jnp.where(rows == r, planes[x][y : y + 1, :], out)
        return out

    ends = [
        jnp.where(quarter < 64, p[:, 0:128], p[:, width - 128 :]) for p in planes[1 : BE - 1]
    ]
    edge = [(x, y) for x in range(1, BE - 1) for y in (0, BE - 1)]
    left = gather(edge[BE:])
    spare = jnp.where(rows_short < 4, left[:, :middle], pltpu.roll(left[:, middle:], 4, 0))
    third = jnp.concatenate(ends[:4], axis=1)
    fourth = jnp.concatenate(ends[4:] + [spare], axis=1)
    return [planes[0], planes[BE - 1], third, fourth, gather(edge[:BE])]


def unpack_shell(tiles):
    width = tiles[0].shape[1]
    quarter, middle = iota((BE, 128), 1), width // 2
    rows = iota((BE, width), 0)
    spare = tiles[3][:, middle:]
    left = jnp.concatenate([spare, pltpu.roll(spare, 4, 0)], axis=1)
    ends = [tiles[2][:, 128 * q : 128 * q + 128] for q in range(4)]
    ends += [tiles[3][:, 128 * q : 128 * q + 128] for q in range(2)]
    planes = [tiles[0]]
    for q, end in enumerate(ends):
        source, r = (tiles[4], 2 * q) if q < 4 else (left, 2 * q - BE)
        low = jnp.where(quarter < 64, end, 0.0)
        high = jnp.where(quarter >= 64, end, 0.0)
        plane = jnp.concatenate([low, jnp.zeros((BE, width - 256), F32), high], axis=1)
        plane = jnp.where(rows == 0, source[r : r + 1, :], plane)
        planes.append(jnp.where(rows == BE - 1, source[r + 1 : r + 2, :], plane))
    return planes + [tiles[1]]


def pack_bricks(source_ref, base, packed_ref):
    def step(t, carry):
        tiles = pack_shell([source_ref[base + t, x].astype(F32) for x in range(BE)])
        for q, tile in enumerate(tiles):
            packed_ref[t, q] = tile.astype(BF16)
        return carry

    lax.fori_loop(0, packed_ref.shape[0], step, 0)


def unpack_arrived(halo, slots, landing_ref, table_ref, base):
    for k, (comes, copy) in enumerate(halo.receives):

        @pl.when(comes)
        def unpack():
            copy.wait_recv()

            def step(t, carry):
                tiles = [landing_ref[t, q].astype(F32) for q in range(5)]
                for x, plane in enumerate(unpack_shell(tiles)):
                    table_ref[base + t, x] = plane.astype(BF16)
                return carry

            lax.fori_loop(slots * k, slots * k + slots, step, 0)


def fill_outbound(send_ref, bricks_ref, out_ref, bricks):
    slots = send_ref.shape[1]
    for k in range(send_ref.shape[0]):
        for s in range(slots):
            out_ref[slots * k + s] = bricks_ref[jnp.minimum(send_ref[k, s], bricks - 1)]


def assemble(table_ref, nbr_ref, shifted_ref):
    width = table_ref.shape[3]
    lanes = iota((BE, 128), 1)
    rows = iota((BE, width + 128), 0)

    def plane(b, direction, source):
        strips = []
        for j in range(3):
            first = direction + 3 * j
            mid = table_ref[nbr_ref[b, first + 1], source].astype(F32)
            low = table_ref[nbr_ref[b, first], source, :, width - 128 : width].astype(F32)
            high = table_ref[nbr_ref[b, first + 2], source, :, 0:128].astype(F32)
            end = mid[:, width - 128 :]
            body = jnp.concatenate(
                [mid[:, : width - 128], jnp.where(lanes >= 64, low, end)], axis=1
            )
            tail = jnp.where(lanes < 64, high, end)
            strips.append(
                jnp.concatenate([pltpu.roll(body, 64, 1), pltpu.roll(tail, 64, 1)], axis=1)
            )
        before = pltpu.roll(jnp.where(rows == BE - 1, strips[0], strips[1]), 1, 0)
        after = pltpu.roll(jnp.where(rows == 0, strips[2], strips[1]), BE - 1, 0)
        return before, strips[1], after

    def step(x, carry):
        side = jnp.where(x == 0, 0, jnp.where(x == BE + 1, 2, 1))
        source = lax.rem(x + BE - 1, BE)
        for pair in range(nbr_ref.shape[0] // 2):
            one = plane(2 * pair, 9 * side, source)
            two = plane(2 * pair + 1, 9 * side, source)
            for j in range(3):
                both = jnp.concatenate([one[j], two[j]], axis=0).astype(BF16)
                shifted_ref[j, x, 16 * pair : 16 * pair + 16, :] = both
        return carry

    lax.fori_loop(0, BE + 2, step, 0)


def band_forward(weight_ref, kernel_ref):
    empty = jnp.zeros((64, 64), F32)
    for n in range(9):
        three = [weight_ref[3 * n + k].astype(F32) for k in range(3)]
        left = jnp.concatenate(three + [empty], axis=0)
        right = jnp.concatenate([empty] + three, axis=0)
        kernel_ref[n] = jnp.concatenate([left, right], axis=1).astype(BF16)


def band_backward(weight_ref, kernel_ref):
    empty = jnp.zeros((64, 64), F32)
    for n in range(9):
        three = [weight_ref[26 - 3 * n - k].astype(F32) for k in range(3)]
        top = jnp.concatenate(three + [empty], axis=1)
        low = jnp.concatenate([empty] + three, axis=1)
        kernel_ref[n] = jnp.concatenate([top, low], axis=0).astype(BF16)


def banded_conv(shifted_ref, kernel_ref, result_ref, first=0, last=None, turned=False):
    length, rows, width = result_ref.shape

    def step(p, carry):
        at = pl.multiple_of(p * 128, 128)
        total = jnp.zeros((length * rows, 128), F32)
        for i in range(3):
            for j in range(3):
                block = shifted_ref[j, i : i + length, :, pl.ds(at, 256)]
                total = total + lax.dot_general(
                    block.reshape(length * rows, 256),
                    kernel_ref[3 * i + j],
                    (((1,), (1 if turned else 0,)), ((), ())),
                    preferred_element_type=F32,
                )
        result_ref[:, :, pl.ds(at, 128)] = total.reshape(length, rows, 128)
        return carry

    lax.fori_loop(first, width // 128 if last is None else last, step, 0)


def banded_grad(shifted_ref, upward, grad_ref):
    rows, width = upward.shape
    turned = [
        upward[:, 128 * p : 128 * p + 128].T.astype(BF16) for p in range(width // 128)
    ]

    def step(i, carry):
        for j in range(3):
            total = jnp.zeros((128, 256), F32)
            for p in range(width // 128):
                block = shifted_ref[j, pl.ds(i, BE), :, 128 * p : 128 * p + 256]
                total = total + jnp.dot(
                    turned[p], block.reshape(rows, 256), preferred_element_type=F32
                )
            flat = total.T
            for k in range(3):
                block = (
                    flat[64 * k : 64 * k + 64, 0:64] + flat[64 * k + 64 : 64 * k + 128, 64:128]
                )
                at = pl.multiple_of(32 * (9 * i + 3 * j + k), 32)
                grad_ref[pl.ds(at, 32), :] = jnp.concatenate([block[0:32], block[32:64]], axis=1)
        return carry

    lax.fori_loop(0, 3, step, 0)


def spread_kernel(nbr_ref, up_ref, mask_ref, weight_ref, own_ref, *rest):
    out_ref, shifted_ref, spread_ref, totals_ref, kernel_ref = rest
    band_backward(weight_ref, kernel_ref)
    bricks, width = own_ref.shape[0], own_ref.shape[3]
    wide = expand_mask(mask_ref)
    up = (to_rows(up_ref) * wide).astype(BF16).astype(F32)
    for j in range(3):
        for x in (0, 1, BE + 2, BE + 3):
            shifted_ref[j, x] = jnp.zeros(shifted_ref.shape[2:], BF16)
    for x in range(BE):
        for b in range(bricks):
            tile = up[x, BE * b : BE * b + BE, :]
            side = jnp.zeros((BE, 128), F32)
            tile = jnp.concatenate([side, tile, side], axis=1)
            tile = jnp.concatenate([tile, jnp.zeros_like(tile)], axis=0)
            for j in range(3):
                moved = pltpu.roll(tile, 2 - j, 0) if j < 2 else tile
                shifted_ref[j, x + 2, 16 * b : 16 * b + 16, :] = moved.astype(BF16)
    banded_conv(shifted_ref, kernel_ref, spread_ref, turned=True)

    def clear(t, carry):
        totals_ref[t] = jnp.zeros(totals_ref.shape[1:], F32)
        return carry

    lax.fori_loop(0, totals_ref.shape[0], clear, 0)
    lanes = iota((BE, 128), 1)
    rows = iota((BE, width), 0)
    rows_short = iota((BE, 128), 0)

    def deposit(x, carry):
        side = jnp.where(x == 0, 0, jnp.where(x == BE + 1, 2, 1))
        target = lax.rem(x + BE - 1, BE)
        for b in range(bricks):
            tile = spread_ref[x, 16 * b : 16 * b + 16, :]
            tile = pltpu.roll(pltpu.roll(tile, width + 64, 1), 15, 0)
            for j in range(3):
                first = 9 * side + 3 * j
                body = tile[0:BE, 0:width] if j == 1 else tile[BE : 2 * BE, 0:width]
                ends = tile[0:BE, width:] if j == 1 else tile[BE : 2 * BE, width:]
                if j != 1:
                    keep = BE - 1 if j == 0 else 0
                    body = jnp.where(rows == keep, body, 0.0)
                    ends = jnp.where(rows_short == keep, ends, 0.0)
                totals_ref[nbr_ref[b, first + 1], target] += body
                totals_ref[nbr_ref[b, first], target, :, width - 128 : width] += jnp.where(
                    lanes >= 64, ends, 0.0
                )
                totals_ref[nbr_ref[b, first + 2], target, :, 0:128] += jnp.where(
                    lanes < 64, ends, 0.0
                )
        return carry

    lax.fori_loop(0, BE + 2, deposit, 0)
    own_ref[...] = totals_ref[0:bricks]
    pack_bricks(totals_ref, bricks, out_ref)


def remote(source, target, sems, index, device):
    return pltpu.make_async_remote_copy(
        src_ref=source,
        dst_ref=target,
        send_sem=sems.at[0, index],
        recv_sem=sems.at[1, index],
        device_id=device,
        device_id_type=pl.DeviceIdType.MESH,
    )


class Halo:
    def __init__(self, owners, slots, sign, source, target, base, sems):
        half = owners // 2
        me = lax.axis_index("space")
        row, column = me // half, me % half
        self.sends, self.receives = [], []
        steps = [(0, -1), (0, 1), (1, -1), (1, 0), (1, 1), (-1, -1), (-1, 0), (-1, 1)]
        for k, (down, right) in enumerate(steps):
            down, right = sign * down, sign * right
            to_row, to_column = row + down, column + right
            from_row, from_column = row - down, column - right
            goes = (to_row >= 0) & (to_row < 2) & (to_column >= 0) & (to_column < half)
            comes = (from_row >= 0) & (from_row < 2) & (from_column >= 0) & (from_column < half)
            device = {"space": (me + down * half + right + owners) % owners}
            copy = remote(
                source.at[slots * k : slots * k + slots],
                target.at[base + slots * k : base + slots * k + slots],
                sems,
                k,
                device,
            )
            self.sends.append((goes, copy))
            self.receives.append((comes, copy))

    def start(self):
        for goes, copy in self.sends:
            pl.when(goes)(copy.start)

    def wait_send(self):
        for goes, copy in self.sends:
            pl.when(goes)(copy.wait_send)


class Total:
    def __init__(self, owners, grad, pair_out, pair_in, mine, out, arrived, full, sems):
        self.owners = owners
        self.me = lax.axis_index("space")
        self.rep = lax.axis_index("rep")
        self.grad, self.pair_out, self.mine, self.out = grad, pair_out, mine, out
        self.pair_in, self.arrived, self.full = pair_in, arrived, full
        self.half = mine.shape[0]
        self.chunk = self.half // owners
        other = {"rep": 1 - self.rep}
        self.pair = remote(pair_out, pair_in, sems, 0, other)
        self.scatter, self.gather_out, self.gather_in = [], [], []
        own = full.at[self.rep, self.rows(self.me), :]
        for s in range(1, owners):
            there = (self.me + s) % owners
            device = {"space": there}
            self.scatter.append(
                remote(out.at[self.rows(there), :], arrived.at[s - 1], sems, s, device)
            )
            landing = full.at[self.rep, self.rows((self.me + owners - s) % owners), :]
            index = owners + s
            self.gather_out.append(remote(own, own, sems, index, device))
            self.gather_in.append(remote(landing, landing, sems, index, device))
        self.share = remote(full.at[self.rep], full.at[self.rep], sems, owners, other)
        coming = full.at[1 - self.rep]
        self.share_in = remote(coming, coming, sems, owners, other)

    def rows(self, owner):
        return pl.ds(pl.multiple_of(owner * self.chunk, self.chunk), self.chunk)

    def halves(self, rep):
        return pl.ds(pl.multiple_of(rep * self.half, self.half), self.half)

    def start_pair(self):
        self.pair_out[...] = self.grad[self.halves(1 - self.rep), :].astype(BF16)
        self.pair.start()

    def start_scatter(self):
        self.pair.wait_recv()
        total = self.grad[self.halves(self.rep), :] + self.pair_in[...].astype(F32)
        self.mine[...] = total
        self.out[...] = total.astype(BF16)
        for copy in self.scatter:
            copy.start()

    def start_gather(self):
        total = self.mine[self.rows(self.me), :]
        for s, copy in enumerate(self.scatter):
            copy.wait_recv()
            total = total + self.arrived[s].astype(F32)
        self.full[self.rep, self.rows(self.me), :] = total.astype(BF16)
        for copy in self.gather_out:
            copy.start()

    def start_share(self):
        for copy in self.gather_in:
            copy.wait_recv()
        self.share.start()

    def finish(self, result_ref):
        self.share_in.wait_recv()
        flat = self.full[...].astype(F32).reshape(2 * self.half, 128)
        for d in range(result_ref.shape[0]):
            block = flat[32 * d : 32 * d + 32]
            result_ref[d, 0:32, :] = block[:, 0:64]
            result_ref[d, 32:64, :] = block[:, 64:128]
        for copy in [self.pair, self.share] + self.scatter + self.gather_out:
            copy.wait_send()


def layers_kernel(
    owners, send_ref, nbr_ref, features_ref, up_ref, mask_ref, one_ref, two_ref, own_ref, terms_ref,
    output_ref, grad_one_ref, grad_two_ref,
    table_ref, x_out, x_in, hidden_out, hidden_in, terms_in, packed_ref, shifted_ref, pre_ref, wide_ref, home_ref,
    bricks_ref, kernel_ref, halo_sems, *rest
):
    bricks = own_ref.shape[0]
    slots = send_ref.shape[1]
    me, rep = lax.axis_index("space"), lax.axis_index("rep")
    barrier = pltpu.get_barrier_semaphore()
    mesh_id = pl.DeviceIdType.MESH
    for s in range(1, owners):
        there = {"space": (me + s) % owners}
        pl.semaphore_signal(barrier, inc=1, device_id=there, device_id_type=mesh_id)
    pl.semaphore_signal(barrier, inc=1, device_id={"rep": 1 - rep}, device_id_type=mesh_id)

    x_halo = Halo(owners, slots, 1, x_out, x_in, 0, halo_sems.at[0])
    back_halo = Halo(owners, slots, -1, terms_ref, terms_in, 0, halo_sems.at[1])
    hidden_halo = Halo(owners, slots, 1, hidden_out, hidden_in, 0, halo_sems.at[2])
    one, two = Total(owners, *rest[:8]), Total(owners, *rest[8:])

    wide_ref[...] = expand_mask(mask_ref)
    for b in range(bricks):
        part = wide_ref[:, BE * b : BE * b + BE, :]
        bricks_ref[b] = (features_ref[b].astype(F32) * part).astype(BF16)
    table_ref[0:bricks] = bricks_ref[...]
    table_ref[table_ref.shape[0] - 1] = jnp.zeros(table_ref.shape[1:], BF16)
    pack_bricks(bricks_ref, 0, packed_ref)
    fill_outbound(send_ref, packed_ref, x_out, bricks)
    pl.semaphore_wait(barrier, owners)
    x_halo.start()
    for total in (one, two):
        size = 32 * grad_one_ref.shape[0]
        total.grad[size:, :] = jnp.zeros((total.grad.shape[0] - size, 128), F32)
    band_forward(one_ref, kernel_ref.at[0])
    band_forward(two_ref, kernel_ref.at[1])
    unpack_arrived(x_halo, slots, x_in, table_ref, bricks)
    back_halo.start()

    assemble(table_ref, nbr_ref, shifted_ref)
    banded_conv(shifted_ref, kernel_ref.at[0], pre_ref)
    pre = pre_ref[...]
    hidden = wide_ref[...] * (pre * jax.nn.sigmoid(pre))
    for b in range(bricks):
        bricks_ref[b] = hidden[:, BE * b : BE * b + BE, :].astype(BF16)
    pack_bricks(bricks_ref, 0, packed_ref)
    fill_outbound(send_ref, packed_ref, hidden_out, bricks)
    hidden_halo.start()
    table_ref[0:bricks] = bricks_ref[...]

    home_ref[...] = own_ref[...]
    for k, (comes, copy) in enumerate(back_halo.receives):

        @pl.when(comes)
        def add_terms():
            copy.wait_recv()

            def step(s, carry):
                tiles = [terms_in[slots * k + s, q].astype(F32) for q in range(5)]
                for x, plane in enumerate(unpack_shell(tiles)):
                    for b in range(bricks):
                        home_ref[b, x] += jnp.where(send_ref[k, s] == b, plane, 0.0)
                return carry

            lax.fori_loop(0, slots, step, 0)

    back = jnp.concatenate([home_ref[b] for b in range(bricks)], axis=1)
    pre = pre_ref[...]
    logistic = jax.nn.sigmoid(pre)
    slope = logistic * (1.0 + pre * (1.0 - logistic))
    inner = (wide_ref[...] * back * slope).astype(BF16).astype(F32)
    banded_grad(shifted_ref, inner.reshape(-1, inner.shape[2]), one.grad)
    one.start_pair()

    unpack_arrived(hidden_halo, slots, hidden_in, table_ref, bricks)
    assemble(table_ref, nbr_ref, shifted_ref)
    one.start_scatter()
    up = (to_rows(up_ref) * wide_ref[...]).astype(BF16).astype(F32)
    banded_grad(shifted_ref, up.reshape(-1, up.shape[2]), two.grad)
    two.start_pair()
    one.start_gather()
    banded_conv(shifted_ref, kernel_ref.at[1], pre_ref, 0, 1)
    two.start_scatter()
    banded_conv(shifted_ref, kernel_ref.at[1], pre_ref, 1, 3)
    one.start_share()
    two.start_gather()
    banded_conv(shifted_ref, kernel_ref.at[1], pre_ref, 3, 4)
    post = pre_ref[...] * wide_ref[...]
    for b in range(bricks):
        output_ref[b] = post[:, BE * b : BE * b + BE, :].astype(BF16)
    one.finish(grad_one_ref)
    two.start_share()
    two.finish(grad_two_ref)
    for halo in (x_halo, back_halo, hidden_halo):
        halo.wait_send()


def call(body, specs, outs, scratch, args, **params):
    return pl.pallas_call(
        body,
        out_shape=outs,
        in_specs=specs,
        out_specs=[VM] * len(outs),
        scratch_shapes=scratch,
        compiler_params=pltpu.CompilerParams(vmem_limit_bytes=LIMIT, **params),
    )(*args)


def per_device(features, weight_one, weight_two, grad_out, active, send_list, local_nbr):
    bricks = features.shape[1]
    width = features.shape[4]
    brick = features.shape[2:]
    send = send_list[0, 0]
    nbr = local_nbr[0]
    owners = lax.axis_size("space")
    slots = send.shape[1]
    mask = active[0].reshape(bricks, BE, BE, BE).transpose(1, 0, 2, 3).reshape(-1, BE)
    shape = jax.ShapeDtypeStruct
    moved = send.shape[0] * slots
    shell = (5, BE, width)
    bricks_half = shape((bricks,) + brick, BF16)
    bricks_full = shape((bricks,) + brick, F32)
    entries = bricks + moved + 1
    rows = bricks * BE
    own_back, terms = call(
        spread_kernel,
        [SM, VM, VM, VM],
        [bricks_full, shape((moved,) + shell, BF16)],
        [
            pltpu.VMEM((3, BE + 4, 16 * bricks, width + 256), BF16),
            pltpu.VMEM((BE + 2, 16 * bricks, width + 128), F32),
            pltpu.VMEM((entries,) + brick, F32),
            pltpu.VMEM((9, 128, 256), BF16),
        ],
        (nbr, grad_out[0], mask, weight_two),
    )
    grads = shape(weight_one.shape, F32)
    chunk = -(-32 * weight_one.shape[0] // (2 * owners * 16)) * 16
    half = owners * chunk
    total = [
        pltpu.VMEM((2 * half, 128), F32),
        pltpu.VMEM((half, 128), BF16),
        pltpu.VMEM((half, 128), BF16),
        pltpu.VMEM((half, 128), F32),
        pltpu.VMEM((half, 128), BF16),
        pltpu.VMEM((owners - 1, chunk, 128), BF16),
        pltpu.VMEM((2, half, 128), BF16),
        pltpu.SemaphoreType.DMA((2, 2 * owners)),
    ]
    table = pltpu.VMEM((entries,) + brick, BF16)
    moving = pltpu.VMEM((moved,) + shell, BF16)
    output, grad_one, grad_two = call(
        functools.partial(layers_kernel, owners),
        [SM, SM] + [VM] * 7,
        [bricks_half, grads, grads],
        [
            table,
            moving,
            moving,
            moving,
            moving,
            moving,
            pltpu.VMEM((bricks,) + shell, BF16),
            pltpu.VMEM((3, BE + 2, rows, width + 128), BF16),
            pltpu.VMEM((BE, rows, width), F32),
            pltpu.VMEM((BE, rows, width), F32),
            pltpu.VMEM((bricks,) + brick, F32),
            pltpu.VMEM((bricks,) + brick, BF16),
            pltpu.VMEM((2, 9, 256, 128), BF16),
            pltpu.SemaphoreType.DMA((3, 2, send.shape[0])),
        ]
        + total
        + total,
        (send, nbr, features[0], grad_out[0], mask, weight_one, weight_two, own_back, terms),
        collective_id=0,
        has_side_effects=True,
    )
    return (output.reshape(features.shape), grad_one, grad_two)


def solution(mesh):
    in_specs = (
        P("rep", ("groups", "space"), None, None, None),
        P(),
        P(),
        P("rep", ("groups", "space"), None, None, None),
        P("rep", ("groups", "space"), None),
        P("rep", ("groups", "space"), None, None),
        P("rep", ("groups", "space"), None),
    )
    out_specs = (
        P("rep", ("groups", "space"), None, None, None),
        P("groups", None, None),
        P("groups", None, None),
    )
    return jax.shard_map(
        per_device, mesh=mesh, in_specs=in_specs, out_specs=out_specs, check_vma=False
    )
```
